128 devices in a mesh: tm: 4 (over x_hi, core), space: 32 (over z, y, x_lo).
Axes of the slice: x: 4 (x_hi: 2, x_lo: 2; x = x_hi * 2 + x_lo), y: 4, z: 4, core: 2. Of those that a mesh axis runs over, the one named last changes fastest.
Arguments:
- connect: int32 [8, 98304], P(None, 'space'), may hold values from 0 to 4355, as said below
- low_face: int32 [34848], P('space'), may hold values from 0 to 4355, as said below
- up_face: int32 [34848], P('space'), may hold values from 0 to 4355, as said below
- strain_map: bfloat16 [48, 24, 98304], P(None, None, 'space'), may hold values from -1.25 to 1.25
- modulus: float32 [98304], P('space'), may hold values from 0.5 to 2
- fluidity: float32 [98304], P('space'), may hold values from 0.02 to 0.24
- element_mass: float32 [98304], P('space'), may hold values from 60 to 240
- forward_strain: bfloat16 [8, 48, 98304], P('tm', None, 'space'), may hold values from -6 to 6
- active: int32 [8, 8, 98304], P('tm', None, 'space'), may hold values 0 or 1
- misfit: float32 [8, 3, 139392], P('tm', None, 'space'), may hold values from -3 to 3
- point_nodal: float32 [4, 3, 139392], P('tm', None, 'space'), may hold values from -5 to 5, as said below
- point_internal: float32 [4, 48, 98304], P('tm', None, 'space'), may hold values from -6 to 6
Outputs:
- coarse_nodal: float32 [4, 3, 139392], P('tm', None, 'space')
- coarse_internal: float32 [4, 48, 98304], P('tm', None, 'space')
- fine_nodal: float32 [4, 3, 139392], P('tm', None, 'space')
- fine_internal: float32 [4, 48, 98304], P('tm', None, 'space')
- sensitivity: float32 [98304], P('space')
The draws below stay inside these ranges and needn't reach their ends.
Inputs may be any that keep to these rules, and one draw needn't show every extreme that they name: `connect`: A partition's nodes form a grid of (32 + 1) x (32 + 1) x (3 + 1) nodes, each grid node one local node. A partition's local element e, with x = e % 32, y = (e // 32) % 32 and z = e // 1024, has as corner c the local node at grid point (x + c % 2, y + (c // 2) % 2, z + c // 4). Entry i of a partition's up_face and entry i of the next partition's low_face are the same physical node; the 1089 entries of one partition are distinct. `up_face`: the 1089 entries of one partition are distinct and match the next partition's low_face entry by entry. `point_nodal`: equal on all copies of a shared node.
All inputs are finite; a program needn't handle non-finite values. No bound on the sum of `active` on one device may be relied on, other than what follows from the above.
Results may differ from the reference program's by a relative error of at most 0.0003.
Values sent between devices are 32-bit elements; how exact they have to be, the bound alone decides.
No kernel may reach another device: no remote copies, remote signals or barrier semaphores. Data moves between devices by JAX's collectives and lax.ppermute only.
A program may use at most 128 MiB of HBM per device.

```python
import math
import jax
import jax.numpy as jnp
from jax import lax

EX = 32
EY = 32
EZ = 3
STEPS = 2
QP = 8
STRAIN = 48
ELEMS_DEV = 3072
NODES_DEV = 4356
FACE = 1089
ELEMS = 98304
NODES = 139392
TIMES = 8
N_TM = 4
N_SPACE = 32


def node_numbers(key):
    partitions = jnp.arange(N_SPACE, dtype=jnp.int32)
    return jax.vmap(lambda partition: jax.random.permutation(jax.random.fold_in(key, partition), NODES_DEV))(partitions)


def corner_nodes():
    element = jnp.arange(ELEMS_DEV, dtype=jnp.int32)
    along_x = element % EX
    along_y = element // EX % EY
    along_z = element // (EX * EY)
    corner = jnp.arange(8, dtype=jnp.int32)
    step_x = (corner % 2)[:, None]
    step_y = (corner // 2 % 2)[:, None]
    step_z = (corner // 4)[:, None]
    return along_x[None] + step_x + (EX + 1) * (along_y[None] + step_y + (EY + 1) * (along_z[None] + step_z))


def draw_connect(key, part):
    numbers = node_numbers(key)
    localized = numbers[:, corner_nodes()]
    return jnp.transpose(localized, (1, 0, 2)).reshape(8, N_SPACE * ELEMS_DEV).astype(jnp.int32)


def draw_low_face(key, part):
    numbers = node_numbers(key)
    return numbers[:, jnp.arange(FACE, dtype=jnp.int32)].reshape(-1).astype(jnp.int32)


def draw_up_face(key, part):
    numbers = node_numbers(key)
    return numbers[:, jnp.arange(FACE, dtype=jnp.int32) + FACE * EZ].reshape(-1).astype(jnp.int32)


def draw_point_nodal(key, part):
    numbers = node_numbers(key)
    key = jax.random.fold_in(key, 7)
    extent = FACE * (EZ * N_SPACE + 1)
    values = jnp.clip(jax.random.normal(key, (N_TM, 3, extent), jnp.float32), -5.0, 5.0)
    structured = jnp.argsort(numbers, axis=1)
    global_index = structured + FACE * EZ * jnp.arange(N_SPACE, dtype=jnp.int32)[:, None]
    localized = values[:, :, global_index]
    return localized.reshape(N_TM, 3, N_SPACE * NODES_DEV).astype(jnp.float32)


def place_ends(values, key, low, high):
    spot = [jax.random.randint(jax.random.fold_in(key, axis), (), 0, length) for axis, length in enumerate(values.shape)]
    widest = values.shape.index(max(values.shape))
    neighbour = spot[:widest] + [(spot[widest] + 1) % values.shape[widest]] + spot[widest + 1:]
    return values.at[tuple(spot)].set(low).at[tuple(neighbour)].set(high)


def levels(stream_key, shape, cuts, smallest, largest):
    def one(position, parts):
        steps = jax.random.uniform(jax.random.fold_in(jax.random.fold_in(stream_key, 6), position), (parts,), jnp.float32, smallest / len(cuts), largest / len(cuts))
        return jnp.repeat(jnp.exp(steps), shape[position] // parts).reshape((-1,) + (1,) * (len(shape) - position - 1))

    level = one(*cuts[0])
    for cut in cuts[1:]:
        level = level * one(*cut)
    return level


def scatter_about(rng, dims, scale, bound, split=(), kind=jnp.bfloat16):
    values = scale * jax.random.normal(rng, dims, jnp.float32)
    if split:
        values = values * levels(rng, dims, split, -0.22, 0.18)
    return jnp.clip(values, -bound, bound).astype(kind)


def setup_inputs(seed: int = 0) -> dict:
    splits = jax.random.split(jax.random.key(seed), 13)
    connect = draw_connect(jax.random.fold_in(splits[12], 71), 0)
    low_face = draw_low_face(jax.random.fold_in(splits[12], 71), 0)
    up_face = draw_up_face(jax.random.fold_in(splits[12], 71), 0)
    strain_map = scatter_about(splits[3], (STRAIN, 24, ELEMS), 24 ** -0.5, 1.25, ((2, 32),))
    modulus = jnp.clip(jnp.exp(math.log(2.0) - 1.3862944 * jax.random.uniform(splits[4], (ELEMS,), jnp.float32) ** levels(splits[4], (ELEMS,), ((0, 32),), -0.2, 0.2)), 0.5, 2.0)
    fluidity = jnp.clip(jnp.exp(math.log(0.24) - 2.4849066 * jax.random.uniform(splits[5], (ELEMS,), jnp.float32) ** levels(splits[5], (ELEMS,), ((0, 32),), -0.2, 0.2)), 0.02, 0.24)
    element_mass = jnp.clip(jnp.exp(math.log(240.0) - 1.3862944 * jax.random.uniform(splits[6], (ELEMS,), jnp.float32) ** levels(splits[6], (ELEMS,), ((0, 32),), -0.2, 0.2)), 60.0, 240.0)
    forward_strain = scatter_about(splits[7], (TIMES, STRAIN, ELEMS), 1.0, 6.0, ((0, 4), (2, 32)))
    active = place_ends((jax.random.randint(splits[8], (TIMES, QP, ELEMS), 0, 2) < 1).astype(jnp.int32), jax.random.fold_in(splits[8], 1), 0, 1)
    misfit = scatter_about(splits[9], (TIMES, 3, NODES), 0.5, 3.0, ((0, 4), (2, 32)), jnp.float32)
    point_nodal = draw_point_nodal(jax.random.fold_in(splits[12], 71), 0)
    point_internal = scatter_about(splits[11], (N_TM, STRAIN, ELEMS), 1.0, 6.0, ((0, 4), (2, 32)), jnp.float32)
    return {"connect": connect, "low_face": low_face, "up_face": up_face, "strain_map": strain_map, "modulus": modulus, "fluidity": fluidity, "element_mass": element_mass, "forward_strain": forward_strain, "active": active, "misfit": misfit, "point_nodal": point_nodal, "point_internal": point_internal}


PRECISE = lax.Precision.HIGHEST
MODULI_PATTERN = (2.0, 2.0, 2.0, 1.0, 1.0, 1.0)


def moduli_rows():
    return jnp.tile(jnp.array(MODULI_PATTERN, jnp.float32), QP)


def driving_term(strain_map, connect, fluidity, active, nodal, internal, inverse_mass):
    scaled = (inverse_mass * nodal)[:, connect].reshape(24, -1)
    rates = fluidity * jnp.repeat(active, 6, axis=0).astype(jnp.float32)
    product = jnp.einsum("rje,je->re", strain_map.astype(jnp.float32), scaled, precision=PRECISE)
    return rates * internal - product


def element_load(strain_map, connect, modulus, driving, node_count):
    forcing = moduli_rows()[:, None] * modulus * driving
    spread = jnp.einsum("rje,re->je", strain_map.astype(jnp.float32), forcing, precision=PRECISE).reshape(3, 8, -1)
    partial_value = jnp.zeros((3, node_count), jnp.float32).at[:, connect].add(spread)
    return forcing, partial_value


def take_part(array, partition, width):
    return lax.dynamic_slice_in_dim(array, partition * width, width, array.ndim - 1)


def flatten_parts(stacked):
    return jnp.transpose(stacked, (1, 0, 2)).reshape(stacked.shape[1], -1)


def share_faces(partials, lows, ups):
    lower = jnp.take_along_axis(partials, lows[:, None, :], axis=2)
    upper = jnp.take_along_axis(partials, ups[:, None, :], axis=2)
    blank = jnp.zeros_like(lower[:1])
    from_below = jnp.concatenate([blank, upper[:-1]], axis=0)
    from_above = jnp.concatenate([lower[1:], blank], axis=0)

    def place(summed, low_index, up_index, below, above):
        return summed.at[:, low_index].add(below).at[:, up_index].add(above)

    return jax.vmap(place)(partials, lows, ups, from_below, from_above)


def reference(connect, low_face, up_face, strain_map, modulus, fluidity, element_mass, forward_strain, active, misfit, point_nodal, point_internal):
    lows = low_face.reshape(N_SPACE, FACE)
    ups = up_face.reshape(N_SPACE, FACE)
    partitions = jnp.arange(N_SPACE, dtype=jnp.int32)

    def mass_part(partition):
        links = take_part(connect, partition, ELEMS_DEV)
        shares = jnp.broadcast_to(take_part(element_mass, partition, ELEMS_DEV) / 8.0, links.shape)
        return jnp.zeros((1, NODES_DEV), jnp.float32).at[0, links].add(shares)

    masses = share_faces(lax.map(mass_part, partitions), lows, ups)
    inverse_mass = 1.0 / flatten_parts(masses)[0]

    def advance(section, nodal, internal):
        def per_partition(partition):
            links = take_part(connect, partition, ELEMS_DEV)
            local_map = take_part(strain_map, partition, ELEMS_DEV)
            driving = driving_term(local_map, links, take_part(fluidity, partition, ELEMS_DEV),
                                   take_part(active[section], partition, ELEMS_DEV),
                                   take_part(nodal, partition, NODES_DEV),
                                   take_part(internal, partition, ELEMS_DEV),
                                   take_part(inverse_mass, partition, NODES_DEV))
            forcing, partial_value = element_load(local_map, links, take_part(modulus, partition, ELEMS_DEV), driving, NODES_DEV)
            partial_value = partial_value + take_part(misfit[section], partition, NODES_DEV)
            stored = take_part(forward_strain[section], partition, ELEMS_DEV).astype(jnp.float32)
            weights = jnp.sum(moduli_rows()[:, None] * driving * stored, axis=0)
            return partial_value, forcing, weights

        partials, forcings, weights = lax.map(per_partition, partitions)
        summed = share_faces(partials, lows, ups)
        return nodal + flatten_parts(summed), internal - flatten_parts(forcings), flatten_parts(weights[:, None, :])[0]

    blank_nodal = jnp.zeros((3, NODES), jnp.float32)
    blank_internal = jnp.zeros((STRAIN, ELEMS), jnp.float32)
    coarse = []
    for window in range(N_TM):
        if window + 1 < N_TM:
            nodal, internal = point_nodal[window + 1], point_internal[window + 1]
        else:
            nodal, internal = blank_nodal, blank_internal
        for section in range(STEPS - 1, -1, -1):
            result = advance(window * STEPS + section, nodal, internal)
            nodal, internal = result[0], result[1]
        coarse.append((nodal, internal))
    fine_nodal = []
    fine_internal = []
    sensitivity = jnp.zeros((ELEMS,), jnp.float32)
    for window in range(N_TM):
        if window + 1 < N_TM:
            nodal, internal = coarse[window + 1]
        else:
            nodal, internal = blank_nodal, blank_internal
        window_nodal = []
        window_internal = []
        for section in range(STEPS - 1, 0, -1):
            nodal, internal, weights = advance(window * STEPS + section, nodal, internal)
            sensitivity = sensitivity + weights
            window_nodal.append(nodal)
            window_internal.append(internal)
        sensitivity = sensitivity + advance(window * STEPS, nodal, internal)[2]
        fine_nodal.extend(window_nodal[::-1])
        fine_internal.extend(window_internal[::-1])
    coarse_nodal = jnp.stack([pair[0] for pair in coarse])
    coarse_internal = jnp.stack([pair[1] for pair in coarse])
    return coarse_nodal, coarse_internal, jnp.stack(fine_nodal), jnp.stack(fine_internal), sensitivity
```

```python
import jax
import jax.numpy as jnp
from jax import lax
from jax.experimental import pallas as pl
from jax.experimental.pallas import tpu as pltpu
from jax.sharding import PartitionSpec as P

LANES = 128
TILES = 24
STRAIN = 48
MAIN_ROWS = 32
GRID_ROWS = 36
ROWS = 40
NODES = 4356
NODE_ROWS = 35
FACE_ROWS = 9
VMEM_LIMIT = 40 * 1024 * 1024

VMEM = pl.BlockSpec(memory_space=pltpu.VMEM)
SMEM = pl.BlockSpec(memory_space=pltpu.SMEM)
F32 = jnp.float32
I32 = jnp.int32


def lane_ids():
    return lax.broadcasted_iota(I32, (8, LANES), 1)


def row_ids():
    return lax.broadcasted_iota(I32, (8, LANES), 0)


def roll(value, shift, axis):
    return pltpu.roll(value, shift % value.shape[axis], axis)


def spread_row(row):
    return jnp.broadcast_to(row, (8, LANES))


def pick(row, lanes):
    return jnp.take_along_axis(spread_row(row), lanes, axis=1)


def lookup(index, rows, row_of, count):
    high, low = index >> 7, index & 127
    found = [jnp.zeros((8, LANES), F32) for _ in range(count)]
    for row in range(rows):
        hit = high == row
        for d in range(count):
            found[d] = jnp.where(hit, pick(row_of(d, row), low), found[d])
    return found


def edge_row(at_x, at_y, at_xy):
    lane, row = lane_ids(), row_ids()
    along_x = jnp.take_along_axis(at_x, (lane & 3) * 32 + 31, axis=1)
    picked = jnp.where((row == (lane >> 2)) & (lane < 32), along_x, 0.0)
    picked = jnp.where((row == 7) & (lane >= 32) & (lane < 64), roll(at_y, -64, 1), picked)
    picked = jnp.where((row == 7) & (lane == 64), roll(at_xy, -63, 1), picked)
    return jnp.sum(picked, axis=0, keepdims=True)


def step_up_x(value):
    return jnp.where((lane_ids() & 31) == 0, 0.0, roll(value, 1, 1))


def step_up_y(value):
    turned = roll(value, 32, 1)
    below = jnp.where(row_ids() == 0, 0.0, roll(turned, 1, 0))
    return jnp.where(lane_ids() < 32, below, turned)


def assemble_plane(t00, t01, t10, t11):
    first = t00 + step_up_x(t01)
    second = t10 + step_up_x(t11)
    main = first + step_up_y(second)
    return main, edge_row(t01 + step_up_y(t11), second, t11)


def corner_planes(main, edge):
    lane, row = lane_ids(), row_ids()
    edge = spread_row(edge)
    along_x = jnp.take_along_axis(edge, row * 4 + (lane >> 5), axis=1)
    moved_x = jnp.where((lane & 31) == 31, along_x, roll(main, -1, 1))

    def move_y(value, last):
        turned = roll(value, -32, 1)
        above = jnp.where(row == 7, last, roll(turned, -1, 0))
        return jnp.where(lane < 96, turned, above)

    return main, moved_x, move_y(main, roll(edge, 64, 1)), move_y(moved_x, roll(edge, 63, 1))


def tables_kernel(connect, faces, mass, table, inverse, face_position, mass_grid, mass_low, mass_up, flat, numbers, onehot):
    for tile in range(TILES):
        flat[pl.ds(tile * 8, 8), :] = connect[:, tile * LANES : (tile + 1) * LANES].astype(F32)
    for plane in range(4):
        base, shift = (plane, 0) if plane < 3 else (2, 4)

        def corner(c):
            return flat[pl.ds(base * 64 + shift + c, 8, stride=8), :]

        numbers[pl.ds(plane * 8, 8), :] = corner(0)
        numbers[pl.ds(MAIN_ROWS + plane, 1), :] = edge_row(corner(1), corner(2), corner(3))
        below = mass[pl.ds((plane - 1) * 8, 8), :] if plane > 0 else 0.0
        above = mass[pl.ds(plane * 8, 8), :] if plane < 3 else 0.0
        both = (below + above) / 8.0
        main, edge = assemble_plane(both, both, both, both)
        mass_grid[pl.ds(plane * 8, 8), :] = main
        mass_grid[pl.ds(MAIN_ROWS + plane, 1), :] = edge
    numbers[pl.ds(GRID_ROWS, 4), :] = jnp.full((4, LANES), -1.0, F32)
    mass_grid[pl.ds(GRID_ROWS, 4), :] = jnp.zeros((4, LANES), F32)
    edges = numbers[pl.ds(MAIN_ROWS, 8), :]
    numbers[pl.ds(MAIN_ROWS, 8), :] = jnp.where((lane_ids() > 64) | (row_ids() > 3), -1.0, edges)
    table[...] = numbers[...].astype(I32)

    rows_at = lax.broadcasted_iota(I32, (ROWS, LANES), 0)
    lanes_at = lax.broadcasted_iota(I32, (LANES, LANES), 0)
    own_lane = lax.broadcasted_iota(I32, (ROWS, LANES), 1).astype(F32)
    found = jnp.zeros((2 * ROWS, LANES), F32)
    for row in range(GRID_ROWS):
        index = table[pl.ds(row, 1), :]
        hit = jnp.broadcast_to(index >> 7, (ROWS, LANES)) == rows_at
        left = jnp.concatenate([jnp.where(hit, float(row), 0.0), jnp.where(hit, own_lane, 0.0)], axis=0)
        right = jnp.where(jnp.broadcast_to(index & 127, (LANES, LANES)) == lanes_at, 1.0, 0.0)
        found = found + lax.dot_general(
            left.astype(jnp.bfloat16), right.astype(jnp.bfloat16), (((1,), (1,)), ((), ())), preferred_element_type=F32
        )
    numbers[...] = found[:ROWS] * 128.0 + found[ROWS:]
    inverse[...] = numbers[...].astype(I32)

    for side in range(2):
        target = (mass_low, mass_up)[side]
        for half in range(2):
            at = pl.ds(half * 8, 8)
            local = faces[side, at, :]
            position = lookup(local, NODE_ROWS, lambda d, row: numbers[pl.ds(row, 1), :], 1)[0]
            position = jnp.where(local < 0, -1, position.astype(I32))
            face_position[side, at, :] = position
            target[at, :] = lookup(position, GRID_ROWS, lambda d, row: mass_grid[pl.ds(row, 1), :], 1)[0]


def loads_kernel(table, face_position, misfit, misfit_grid, face_inverse, source):
    for section in range(2):
        for d in range(3):
            source[d, pl.ds(32, 8), :] = jnp.zeros((8, LANES), F32)
            for row in range(NODE_ROWS):
                width = min(LANES, NODES - row * LANES)
                source[d, pl.ds(row, 1), :width] = misfit[d, pl.ds(section, 1), row * LANES : row * LANES + width]
        for block in range(5):
            at = pl.ds(block * 8, 8)
            found = lookup(table[at, :], NODE_ROWS, lambda d, row: source[d, pl.ds(row, 1), :], 3)
            for d in range(3):
                misfit_grid[section, d, at, :] = found[d]
    rows_at = lax.broadcasted_iota(I32, (ROWS, LANES), 0)
    lanes_at = lax.broadcasted_iota(I32, (LANES, LANES), 0)
    own_lane = lax.broadcasted_iota(I32, (ROWS, LANES), 1).astype(F32)
    for side in range(2):
        found = jnp.zeros((2 * ROWS, LANES), F32)
        for row in range(FACE_ROWS):
            index = face_position[side, pl.ds(row, 1), :]
            hit = jnp.broadcast_to(index >> 7, (ROWS, LANES)) == rows_at
            left = jnp.concatenate([jnp.where(hit, float(row + 1), 0.0), jnp.where(hit, own_lane, 0.0)], axis=0)
            right = jnp.where(jnp.broadcast_to(index & 127, (LANES, LANES)) == lanes_at, 1.0, 0.0)
            found = found + lax.dot_general(
                left.astype(jnp.bfloat16), right.astype(jnp.bfloat16), (((1,), (1,)), ((), ())), preferred_element_type=F32
            )
        face_inverse[side] = ((found[:ROWS] - 1.0) * 128.0 + found[ROWS:]).astype(I32)


def face_terms(face_inverse, at, from_low, from_up, keep_low, keep_up, count):
    low = lookup(face_inverse[0, at, :], FACE_ROWS, from_low, count)
    up = lookup(face_inverse[1, at, :], FACE_ROWS, from_up, count)
    return [low[d] * keep_low + up[d] * keep_up for d in range(count)]


def gather_corners(scaled, corners):
    for d in range(3):
        for plane in range(4):
            shifted = corner_planes(scaled[d, pl.ds(plane * 8, 8), :], scaled[d, pl.ds(MAIN_ROWS + plane, 1), :])
            for up in range(2):
                layer = plane - up
                if 0 <= layer < 3:
                    for c in range(4):
                        corners[d, pl.ds(layer * 64 + up * 4 + c, 8, stride=8), :] = shifted[c]


def assemble(spread, misfit_grid, section, partial):
    for d in range(3):
        edges = []
        for plane in range(4):
            terms = []
            for c in range(4):
                total = None
                for up in range(2):
                    layer = plane - up
                    if 0 <= layer < 3:
                        term = spread[d, pl.ds(layer * 64 + up * 4 + c, 8, stride=8), :]
                        total = term if total is None else total + term
                terms.append(total)
            main, edge = assemble_plane(*terms)
            at = pl.ds(plane * 8, 8)
            partial[d, at, :] = main + misfit_grid[section, d, at, :]
            edges.append(edge)
        at = pl.ds(MAIN_ROWS, 8)
        edges = jnp.concatenate(edges + [jnp.zeros((4, LANES), F32)], axis=0)
        partial[d, at, :] = edges + misfit_grid[section, d, at, :]


def moduli_column(block):
    row = (row_ids() + block * 8) % 6
    return jnp.where(row < 3, 2.0, 1.0)


def element_sweep(section, load, weigh, strain_map, modulus, fluidity, active, stored, internal, corners,
                  keep, internal_out, spread, weight, sums, rows):
    def tile_step(tile, carry):
        lanes = pl.ds(pl.multiple_of(tile * LANES, LANES), LANES)
        here = pl.ds(pl.multiple_of(tile * 8, 8), 8)
        scaled = [corners[d, here, :] for d in range(3)]
        rate = active[section, :, lanes].astype(F32) * fluidity[pl.ds(tile, 1), :]
        stiffness = modulus[pl.ds(tile, 1), :]
        total = [jnp.zeros((8, LANES), F32) for _ in range(3)]
        heavy = jnp.zeros((8, LANES), F32)
        for block in range(6):
            for i in range(8):
                lines = strain_map[block * 8 + i, :, lanes].astype(F32)
                sums[block, pl.ds(i * 8, 8), :] = lines[0:8] * scaled[0] + lines[8:16] * scaled[1] + lines[16:24] * scaled[2]
            product = sums[block, pl.ds(0, 8, stride=8), :]
            for i in range(1, 8):
                product = product + sums[block, pl.ds(i, 8, stride=8), :]
            point = block * 8 // 6
            rates = jnp.where(row_ids() + block * 8 < (point + 1) * 6, rate[point : point + 1], rate[point + 1 : point + 2])
            rows_here = pl.ds(block * 8, 8)
            held = internal[rows_here, lanes]
            if keep is not None:
                held = held * keep
            driving = rates * held - product
            scaled_driving = moduli_column(block) * driving
            if weigh:
                heavy = heavy + scaled_driving * stored[section, rows_here, lanes].astype(F32)
            if load:
                forcing = stiffness * scaled_driving
                internal_out[rows_here, lanes] = held - forcing
                rows[rows_here, :] = forcing
                for i in range(8):
                    lines = strain_map[block * 8 + i, :, lanes].astype(F32)
                    row = spread_row(rows[pl.ds(block * 8 + i, 1), :])
                    for d in range(3):
                        total[d] = total[d] + lines[d * 8 : d * 8 + 8] * row
        if load:
            for d in range(3):
                spread[d, here, :] = total[d]
        if weigh:
            weight[pl.ds(tile, 1), :] = jnp.sum(heavy, axis=0, keepdims=True)
        return carry

    lax.fori_loop(0, TILES, tile_step, 0)


def send_faces(face_position, partial, face_low, face_up):
    for side, target in ((0, face_low), (1, face_up)):
        for half in range(2):
            at = pl.ds(half * 8, 8)
            found = lookup(face_position[side, at, :], GRID_ROWS, lambda d, row: partial[d, pl.ds(row, 1), :], 3)
            for d in range(3):
                target[d, at, :] = found[d]


def sum_faces(nodal, partial, face_inverse, from_low, from_up, flags, result):
    for block in range(5):
        at = pl.ds(block * 8, 8)
        extra = face_terms(face_inverse, at, lambda d, row: from_low[d, pl.ds(row, 1), :],
                           lambda d, row: from_up[d, pl.ds(row, 1), :], flags[1], flags[2], 3)
        for d in range(3):
            result[d, at, :] = nodal[d, at, :] + (partial[d, at, :] + extra[d])


def first_kernel(flags, mass_grid, from_low, from_up, face_inverse, face_position, table, nodal, internal, strain_map,
                 modulus, fluidity, active, misfit_grid,
                 inverse_mass, nodal_grid, partial, face_low, face_up, internal_out,
                 source, scaled, corners, spread, sums, rows):
    for d in range(3):
        source[d, pl.ds(32, 8), :] = jnp.zeros((8, LANES), F32)
        for row in range(NODE_ROWS):
            width = min(LANES, NODES - row * LANES)
            source[d, pl.ds(row, 1), :width] = nodal[d, :, row * LANES : row * LANES + width]
    keep = flags[0]
    for block in range(5):
        at = pl.ds(block * 8, 8)
        extra = face_terms(face_inverse, at, lambda d, row: from_low[pl.ds(row, 1), :],
                           lambda d, row: from_up[pl.ds(row, 1), :], flags[1], flags[2], 1)[0]
        mass = mass_grid[at, :] + extra
        inverse = 1.0 / jnp.where(table[at, :] < 0, 1.0, mass)
        inverse_mass[at, :] = inverse
        found = lookup(table[at, :], NODE_ROWS, lambda d, row: source[d, pl.ds(row, 1), :], 3)
        for d in range(3):
            value = found[d] * keep
            nodal_grid[d, at, :] = value
            scaled[d, at, :] = value * inverse
    gather_corners(scaled, corners)
    element_sweep(1, True, False, strain_map, modulus, fluidity, active, None, internal, corners, keep,
                  internal_out, spread, None, sums, rows)
    assemble(spread, misfit_grid, 1, partial)
    send_faces(face_position, partial, face_low, face_up)


def second_kernel(flags, nodal, partial, from_low, from_up, face_inverse, face_position, inverse_mass, internal,
                  strain_map, modulus, fluidity, active, misfit_grid,
                  nodal_grid, partial_out, face_low, face_up, internal_out,
                  scaled, corners, spread, sums, rows):
    sum_faces(nodal, partial, face_inverse, from_low, from_up, flags, nodal_grid)
    for d in range(3):
        scaled[d] = nodal_grid[d] * inverse_mass[...]
    gather_corners(scaled, corners)
    element_sweep(0, True, False, strain_map, modulus, fluidity, active, None, internal, corners, None,
                  internal_out, spread, None, sums, rows)
    assemble(spread, misfit_grid, 0, partial_out)
    send_faces(face_position, partial_out, face_low, face_up)


def finish_kernel(flags, nodal, partial, from_low, from_up, face_inverse, nodal_grid):
    sum_faces(nodal, partial, face_inverse, from_low, from_up, flags, nodal_grid)


def third_kernel(flags, nodal, face_position, inverse_mass, internal, strain_map, modulus, fluidity, active, stored,
                 misfit_grid, nodal_grid, partial, face_low, face_up, internal_out, weight,
                 scaled, corners, spread, sums, rows):
    for d in range(3):
        value = nodal[d] * flags[0]
        nodal_grid[d] = value
        scaled[d] = value * inverse_mass[...]
    gather_corners(scaled, corners)
    element_sweep(1, True, True, strain_map, modulus, fluidity, active, stored, internal, corners, flags[0],
                  internal_out, spread, weight, sums, rows)
    assemble(spread, misfit_grid, 1, partial)
    send_faces(face_position, partial, face_low, face_up)


def last_kernel(flags, nodal, partial, from_low, from_up, face_inverse, inverse_mass, internal, strain_map,
                fluidity, active, stored, weight_in, modulus, nodal_grid, weight, scaled, corners, sums):
    sum_faces(nodal, partial, face_inverse, from_low, from_up, flags, nodal_grid)
    for d in range(3):
        scaled[d] = nodal_grid[d] * inverse_mass[...]
    gather_corners(scaled, corners)
    element_sweep(0, False, True, strain_map, modulus, fluidity, active, stored, internal, corners, None,
                  None, None, weight, sums, None)
    weight[...] = weight[...] + weight_in[...]


def local_kernel(inverse, nodal_grid, nodal, found_rows):
    for block in range(5):
        at = pl.ds(block * 8, 8)
        found = lookup(inverse[at, :], GRID_ROWS, lambda d, row: nodal_grid[d, pl.ds(row, 1), :], 3)
        for d in range(3):
            found_rows[d, at, :] = found[d]
    for d in range(3):
        for row in range(NODE_ROWS):
            width = min(LANES, NODES - row * LANES)
            nodal[d, :, row * LANES : row * LANES + width] = found_rows[d, pl.ds(row, 1), :width]


def shape(*dims, dtype=F32):
    return jax.ShapeDtypeStruct(dims, dtype)


def call(kernel, outs, scratch, flagged, *operands, name=None):
    specs = [VMEM] * len(operands)
    if flagged:
        specs[0] = SMEM
    return pl.pallas_call(
        kernel,
        in_specs=specs,
        out_specs=jax.tree.map(lambda _: VMEM, outs),
        out_shape=outs,
        scratch_shapes=scratch,
        compiler_params=pltpu.CompilerParams(vmem_limit_bytes=VMEM_LIMIT),
        name=name,
    )(*operands)


NODAL = (3, ROWS, LANES)
FACES = (3, 16, LANES)


def vm(*dims, dtype=F32):
    return pltpu.VMEM(dims, dtype)


def exchange(low, up):
    count = lax.axis_size("space")
    forward = [(i, (i + 1) % count) for i in range(count)]
    backward = [((i + 1) % count, i) for i in range(count)]
    return lax.ppermute(up, "space", forward), lax.ppermute(low, "space", backward)


def to_earlier(block):
    count = lax.axis_size("tm")
    return lax.ppermute(block, "tm", [((i + 1) % count, i) for i in range(count)])


def sum_windows(value):
    count = lax.axis_size("tm")
    value = value + lax.ppermute(value, "tm", [(i, i ^ 1) for i in range(count)])
    return value + lax.ppermute(value, "tm", [(i, i ^ 2) for i in range(count)])


def per_device(connect, low_face, up_face, strain_map, modulus, fluidity, element_mass, forward_strain, active, misfit,
               point_nodal, point_internal):
    window, place = lax.axis_index("tm"), lax.axis_index("space")
    flags = jnp.stack([
        window < lax.axis_size("tm") - 1, place > 0, place < lax.axis_size("space") - 1
    ]).astype(F32)
    modulus = modulus.reshape(TILES, LANES)
    fluidity = fluidity.reshape(TILES, LANES)
    mass = element_mass.reshape(TILES, LANES)
    faces = jnp.stack([low_face, up_face])
    faces = jnp.pad(faces, ((0, 0), (0, 16 * LANES - faces.shape[1])), constant_values=-1).reshape(2, 16, LANES)
    nodal = to_earlier(jnp.transpose(point_nodal, (1, 0, 2)))
    internal = to_earlier(point_internal[0])
    table, inverse, face_position, mass_grid, mass_low, mass_up = call(
        tables_kernel,
        (shape(ROWS, LANES, dtype=I32), shape(ROWS, LANES, dtype=I32), shape(2, 16, LANES, dtype=I32),
         shape(ROWS, LANES), shape(16, LANES), shape(16, LANES)),
        [vm(TILES * 8, LANES), vm(ROWS, LANES), vm(8, LANES)],
        False, connect, faces, mass, name="tables",
    )
    from_low, from_up = exchange(mass_low, mass_up)
    misfit_grid, face_inverse = call(
        loads_kernel, (shape(2, *NODAL), shape(2, ROWS, LANES, dtype=I32)), [vm(*NODAL)],
        False, table, face_position, jnp.transpose(misfit, (1, 0, 2)), name="loads",
    )
    work = [vm(*NODAL), vm(3, TILES * 8, LANES), vm(3, TILES * 8, LANES), vm(6, 64, LANES), vm(STRAIN, LANES)]
    moved = (shape(*NODAL), shape(*NODAL), shape(*FACES), shape(*FACES), shape(STRAIN, TILES * LANES))
    inverse_mass, nodal, partial, face_low, face_up, internal = call(
        first_kernel, (shape(ROWS, LANES),) + moved, [vm(*NODAL)] + work,
        True, flags, mass_grid, from_low, from_up, face_inverse, face_position, table, nodal, internal, strain_map,
        modulus, fluidity, active, misfit_grid, name="first",
    )
    from_low, from_up = exchange(face_low, face_up)
    nodal, partial, face_low, face_up, coarse_internal = call(
        second_kernel, moved, work,
        True, flags, nodal, partial, from_low, from_up, face_inverse, face_position, inverse_mass, internal, strain_map,
        modulus, fluidity, active, misfit_grid, name="second",
    )
    internal = to_earlier(coarse_internal)
    from_low, from_up = exchange(face_low, face_up)
    coarse = call(finish_kernel, shape(*NODAL), [], True, flags, nodal, partial, from_low, from_up, face_inverse, name="finish")
    nodal = to_earlier(coarse)

    def to_local(grid):
        local = call(local_kernel, shape(3, 1, NODES), [vm(*NODAL)], False, inverse, grid, name="local")
        return jnp.transpose(local, (1, 0, 2))

    coarse_nodal = to_local(coarse)
    nodal, partial, face_low, face_up, fine_internal, weight = call(
        third_kernel, moved + (shape(TILES, LANES),), work,
        True, flags, nodal, face_position, inverse_mass, internal, strain_map, modulus, fluidity, active, forward_strain,
        misfit_grid, name="third",
    )
    from_low, from_up = exchange(face_low, face_up)
    fine, weight = call(
        last_kernel, (shape(*NODAL), shape(TILES, LANES)), [vm(*NODAL), vm(3, TILES * 8, LANES), vm(6, 64, LANES)],
        True, flags, nodal, partial, from_low, from_up, face_inverse, inverse_mass, fine_internal, strain_map,
        fluidity, active, forward_strain, weight, modulus, name="last",
    )
    sensitivity = sum_windows(weight)
    fine_nodal = to_local(fine)
    return coarse_nodal, coarse_internal[None], fine_nodal, fine_internal[None], sensitivity.reshape(-1)


def solution(mesh):
    in_specs = (
        P(None, "space"), P("space"), P("space"), P(None, None, "space"), P("space"), P("space"), P("space"),
        P("tm", None, "space"), P("tm", None, "space"), P("tm", None, "space"), P("tm", None, "space"),
        P("tm", None, "space"),
    )
    out_specs = (
        P("tm", None, "space"), P("tm", None, "space"), P("tm", None, "space"), P("tm", None, "space"), P("space"),
    )
    return jax.shard_map(per_device, mesh=mesh, in_specs=in_specs, out_specs=out_specs, check_vma=False)
```

```python
import jax
import jax.numpy as jnp
from jax import lax
from jax.experimental import pallas as pl
from jax.experimental.pallas import tpu as pltpu
from jax.sharding import PartitionSpec as P

LANES = 128
TILES = 24
STRAIN = 48
MAIN_ROWS = 32
GRID_ROWS = 36
ROWS = 40
NODES = 4356
NODE_ROWS = 35
FACE_ROWS = 9
VMEM_LIMIT = 12 * 1024 * 1024

VMEM = pl.BlockSpec(memory_space=pltpu.VMEM)
HBM = pl.BlockSpec(memory_space=pltpu.HBM)
F32 = jnp.float32
I32 = jnp.int32


def fetch(sources, targets, arrived):
    copies = [pltpu.make_async_copy(source, target, arrived.at[i]) for i, (source, target) in enumerate(zip(sources, targets))]
    for copy in copies:
        copy.start()
    return copies


def lane_ids():
    return lax.broadcasted_iota(I32, (8, LANES), 1)


def row_ids():
    return lax.broadcasted_iota(I32, (8, LANES), 0)


def roll(value, shift, axis):
    return pltpu.roll(value, shift % value.shape[axis], axis)


def spread_row(row):
    return jnp.broadcast_to(row, (8, LANES))


def pick(row, lanes):
    return jnp.take_along_axis(spread_row(row), lanes, axis=1)


def lookup(index, rows, row_of, count):
    high, low = index >> 7, index & 127
    found = [jnp.zeros((8, LANES), F32) for _ in range(count)]
    for row in range(rows):
        hit = high == row
        for d in range(count):
            found[d] = jnp.where(hit, pick(row_of(d, row), low), found[d])
    return found


def edge_row(at_x, at_y, at_xy):
    lane, row = lane_ids(), row_ids()
    along_x = jnp.take_along_axis(at_x, (lane & 3) * 32 + 31, axis=1)
    picked = jnp.where((row == (lane >> 2)) & (lane < 32), along_x, 0.0)
    picked = jnp.where((row == 7) & (lane >= 32) & (lane < 64), roll(at_y, -64, 1), picked)
    picked = jnp.where((row == 7) & (lane == 64), roll(at_xy, -63, 1), picked)
    return jnp.sum(picked, axis=0, keepdims=True)


def step_up_x(value):
    return jnp.where((lane_ids() & 31) == 0, 0.0, roll(value, 1, 1))


def step_up_y(value):
    turned = roll(value, 32, 1)
    below = jnp.where(row_ids() == 0, 0.0, roll(turned, 1, 0))
    return jnp.where(lane_ids() < 32, below, turned)


def assemble_plane(t00, t01, t10, t11):
    first = t00 + step_up_x(t01)
    second = t10 + step_up_x(t11)
    main = first + step_up_y(second)
    return main, edge_row(t01 + step_up_y(t11), second, t11)


def corner_planes(main, edge):
    lane, row = lane_ids(), row_ids()
    edge = spread_row(edge)
    along_x = jnp.take_along_axis(edge, row * 4 + (lane >> 5), axis=1)
    moved_x = jnp.where((lane & 31) == 31, along_x, roll(main, -1, 1))

    def move_y(value, last):
        turned = roll(value, -32, 1)
        above = jnp.where(row == 7, last, roll(turned, -1, 0))
        return jnp.where(lane < 96, turned, above)

    return main, moved_x, move_y(main, roll(edge, 64, 1)), move_y(moved_x, roll(edge, 63, 1))


def even_place():
    return lax.axis_index("space") % 2 == 0


def has_earlier_state():
    return jnp.where(lax.axis_index("tm") < lax.axis_size("tm") - 1, 1.0, 0.0)


def has_far_face():
    place = lax.axis_index("space")
    return jnp.where((place > 0) & (place < lax.axis_size("space") - 1), 1.0, 0.0)


def tables_kernel(connect_in, low_in, up_in, mass_in, table, inverse, face_position, mass_grid, mass_near, mass_far,
                  flat, numbers, faces, connect, low_face, up_face, mass, arrived):
    copies = fetch((connect_in, low_in, up_in, mass_in), (connect, low_face, up_face, mass), arrived)
    even = even_place()
    faces[...] = jnp.full((24, LANES), -1, I32)
    for copy in copies:
        copy.wait()
    for row in range(FACE_ROWS):
        width = min(LANES, low_face.shape[0] - row * LANES)
        at = slice(row * LANES, row * LANES + width)
        low, up = low_face[at], up_face[at]
        near, far = jnp.where(even, up, low), jnp.where(even, low, up)
        to = (row, row + 8) if row < 8 else (16, 17)
        faces[to[0], :width] = near
        faces[to[1], :width] = far
    for tile in range(TILES):
        flat[pl.ds(tile * 8, 8), :] = connect[:, tile * LANES : (tile + 1) * LANES].astype(F32)
    for plane in range(4):
        base, shift = (plane, 0) if plane < 3 else (2, 4)

        def corner(c):
            return flat[pl.ds(base * 64 + shift + c, 8, stride=8), :]

        numbers[pl.ds(plane * 8, 8), :] = corner(0)
        numbers[pl.ds(MAIN_ROWS + plane, 1), :] = edge_row(corner(1), corner(2), corner(3))
        below = mass[pl.ds((plane - 1) * 8, 8), :] if plane > 0 else 0.0
        above = mass[pl.ds(plane * 8, 8), :] if plane < 3 else 0.0
        both = (below + above) / 8.0
        main, edge = assemble_plane(both, both, both, both)
        mass_grid[pl.ds(plane * 8, 8), :] = main
        mass_grid[pl.ds(MAIN_ROWS + plane, 1), :] = edge
    numbers[pl.ds(GRID_ROWS, 4), :] = jnp.full((4, LANES), -1.0, F32)
    mass_grid[pl.ds(GRID_ROWS, 4), :] = jnp.zeros((4, LANES), F32)
    edges = numbers[pl.ds(MAIN_ROWS, 8), :]
    numbers[pl.ds(MAIN_ROWS, 8), :] = jnp.where((lane_ids() > 64) | (row_ids() > 3), -1.0, edges)
    table[...] = numbers[...].astype(I32)

    rows_at = lax.broadcasted_iota(I32, (ROWS, LANES), 0)
    lanes_at = lax.broadcasted_iota(I32, (LANES, LANES), 0)
    own_lane = lax.broadcasted_iota(I32, (ROWS, LANES), 1).astype(F32)
    found = jnp.zeros((2 * ROWS, LANES), F32)
    for row in range(GRID_ROWS):
        index = table[pl.ds(row, 1), :]
        hit = jnp.broadcast_to(index >> 7, (ROWS, LANES)) == rows_at
        left = jnp.concatenate([jnp.where(hit, float(row), 0.0), jnp.where(hit, own_lane, 0.0)], axis=0)
        right = jnp.where(jnp.broadcast_to(index & 127, (LANES, LANES)) == lanes_at, 1.0, 0.0)
        found = found + lax.dot_general(
            left.astype(jnp.bfloat16), right.astype(jnp.bfloat16), (((1,), (1,)), ((), ())), preferred_element_type=F32
        )
    numbers[...] = found[:ROWS] * 128.0 + found[ROWS:]
    inverse[...] = numbers[...].astype(I32)

    found = []
    for block in range(3):
        at = pl.ds(block * 8, 8)
        local = faces[at, :]
        position = lookup(local, NODE_ROWS, lambda d, row: numbers[pl.ds(row, 1), :], 1)[0]
        position = jnp.where(local < 0, -1, position.astype(I32))
        face_position[at, :] = position
        found.append(lookup(position, GRID_ROWS, lambda d, row: mass_grid[pl.ds(row, 1), :], 1))
    put_faces(found, mass_near, mass_far, 1)


def put_faces(found, near, far, count):
    for d in range(count):
        near[pl.ds(d * 16, 8), :] = found[0][d]
        near[pl.ds(d * 16 + 8, 8), :] = found[2][d]
        far[pl.ds(d * 16, 8), :] = found[1][d]
        far[pl.ds(d * 16 + 8, 8), :] = roll(found[2][d], -1, 0)


def local_to_grid(source, local, rows, table, put):
    for d in range(3):
        source[d, pl.ds(32, 8), :] = jnp.zeros((8, LANES), F32)
        for row in range(NODE_ROWS):
            width = min(LANES, NODES - row * LANES)
            source[d, pl.ds(row, 1), :width] = local[d, rows, row * LANES : row * LANES + width]
    for block in range(5):
        at = pl.ds(block * 8, 8)
        put(at, lookup(table[at, :], NODE_ROWS, lambda d, row: source[d, pl.ds(row, 1), :], 3))


def loads_kernel(table, face_position, misfit_in, nodal, misfit_grid, face_inverse, nodal_grid, source, misfit, arrived):
    copies = fetch((misfit_in,), (misfit,), arrived)
    keep = has_earlier_state()

    def put_nodal(at, found):
        for d in range(3):
            nodal_grid[d, at, :] = found[d] * keep

    local_to_grid(source, nodal, pl.ds(0, 1), table, put_nodal)
    copies[0].wait()
    for section in range(2):

        def put(at, found):
            for d in range(3):
                misfit_grid[section, d, at, :] = found[d]

        local_to_grid(source, misfit, pl.ds(section, 1), table, put)
    rows_at = lax.broadcasted_iota(I32, (ROWS, LANES), 0)
    lanes_at = lax.broadcasted_iota(I32, (LANES, LANES), 0)
    own_lane = lax.broadcasted_iota(I32, (ROWS, LANES), 1).astype(F32)
    for side in range(2):
        found = jnp.zeros((2 * ROWS, LANES), F32)
        for row in range(FACE_ROWS):
            index = face_position[pl.ds(row + side * 8 if row < 8 else 16 + side, 1), :]
            hit = jnp.broadcast_to(index >> 7, (ROWS, LANES)) == rows_at
            left = jnp.concatenate([jnp.where(hit, float(row + 1), 0.0), jnp.where(hit, own_lane, 0.0)], axis=0)
            right = jnp.where(jnp.broadcast_to(index & 127, (LANES, LANES)) == lanes_at, 1.0, 0.0)
            found = found + lax.dot_general(
                left.astype(jnp.bfloat16), right.astype(jnp.bfloat16), (((1,), (1,)), ((), ())), preferred_element_type=F32
            )
        face_inverse[side] = ((found[:ROWS] - 1.0) * 128.0 + found[ROWS:]).astype(I32)


CHUNKS = 6


def widen_kernel(strain_map, modulus_in, fluidity_in, active_in, wide_map, stiffness, decay, softness,
                 narrow, modulus, fluidity, active, arrived, small_arrived):
    depth = STRAIN // CHUNKS
    small = fetch((modulus_in, fluidity_in, active_in), (modulus, fluidity, active), small_arrived)
    copies = fetch(
        [strain_map.at[pl.ds(part * depth, depth)] for part in range(CHUNKS)], [narrow.at[part] for part in range(CHUNKS)], arrived
    )
    for copy in small:
        copy.wait()
    softness[...] = 1.0 / modulus[...]

    def tile_step(tile, carry):
        lanes = pl.ds(pl.multiple_of(tile * LANES, LANES), LANES)
        own = spread_row(modulus[pl.ds(tile, 1), :])
        rates = [active[n, :, lanes].astype(F32) * fluidity[pl.ds(tile, 1), :] for n in range(2)]
        for block in range(6):
            row = row_ids() + block * 8
            here = jnp.where(row % 6 < 3, 2.0, 1.0) * own
            stiffness[pl.ds(block * 8, 8), lanes] = here
            point = block * 8 // 6
            for n in range(2):
                rate = jnp.where(row < (point + 1) * 6, rates[n][point : point + 1], rates[n][point + 1 : point + 2])
                decay[n, pl.ds(block * 8, 8), lanes] = here * rate
        return carry

    lax.fori_loop(0, TILES, tile_step, 0)
    for part in range(CHUNKS):
        copies[part].wait()

        def row_step(row, carry):
            to = pl.ds(pl.multiple_of((part * depth + row) * 24, 8), 24)
            for tile in range(TILES):
                wide_map[tile, to, :] = narrow[part, row, :, tile * LANES : (tile + 1) * LANES].astype(F32)
            return carry

        lax.fori_loop(0, depth, row_step, 0)


def face_terms(face_inverse, at, near, far, count):
    from_near = lookup(face_inverse[0, at, :], FACE_ROWS, lambda d, row: near[pl.ds(d * 16 + row, 1), :], count)
    from_far = lookup(face_inverse[1, at, :], FACE_ROWS, lambda d, row: far[pl.ds(d * 16 + row, 1), :], count)
    keep = has_far_face()
    return [from_near[d] + from_far[d] * keep for d in range(count)]


def gather_corners(scaled, corners):
    for d in range(3):
        for plane in range(4):
            shifted = corner_planes(scaled[d, pl.ds(plane * 8, 8), :], scaled[d, pl.ds(MAIN_ROWS + plane, 1), :])
            for up in range(2):
                layer = plane - up
                if 0 <= layer < 3:
                    for c in range(4):
                        corners[d, pl.ds(layer * 64 + up * 4 + c, 8, stride=8), :] = shifted[c]


def assemble(spread, misfit_grid, section, partial):
    for d in range(3):
        edges = []
        for plane in range(4):
            terms = []
            for c in range(4):
                total = None
                for up in range(2):
                    layer = plane - up
                    if 0 <= layer < 3:
                        term = spread[d, pl.ds(layer * 64 + up * 4 + c, 8, stride=8), :]
                        total = term if total is None else total + term
                terms.append(total)
            main, edge = assemble_plane(*terms)
            at = pl.ds(plane * 8, 8)
            partial[d, at, :] = main + misfit_grid[section, d, at, :]
            edges.append(edge)
        at = pl.ds(MAIN_ROWS, 8)
        edges = jnp.concatenate(edges + [jnp.zeros((4, LANES), F32)], axis=0)
        partial[d, at, :] = edges + misfit_grid[section, d, at, :]


PITCH = 9
TOGETHER = 2


def element_sweep(section, load, weigh, wide_map, softness, stiffness, decay, stored, internal, corners,
                  keep, internal_out, spread, weight, sums, rows):
    def tile_step(tile, slot):
        lanes = pl.ds(pl.multiple_of(tile * LANES, LANES), LANES)
        here = pl.ds(pl.multiple_of(tile * 8, 8), 8)
        scaled = [corners[d, here, :] for d in range(3)]
        total = [jnp.zeros((8, LANES), F32) for _ in range(3)]
        heavy = jnp.zeros((8, LANES), F32)
        for block in range(6):
            for i in range(8):
                lines = wide_map[tile, pl.ds((block * 8 + i) * 24, 24), :]
                sums[slot * 6 + block][pl.ds(i * PITCH, 8), :] = (
                    lines[0:8] * scaled[0] + lines[8:16] * scaled[1] + lines[16:24] * scaled[2]
                )
            product = sums[slot * 6 + block][pl.ds(0, 8, stride=PITCH), :]
            for i in range(1, 8):
                product = product + sums[slot * 6 + block][pl.ds(i, 8, stride=PITCH), :]
            rows_here = pl.ds(block * 8, 8)
            held = internal[rows_here, lanes]
            if keep is not None:
                held = held * keep
            forcing = decay[section, rows_here, lanes] * held - stiffness[rows_here, lanes] * product
            if weigh:
                heavy = heavy + forcing * stored[rows_here, lanes].astype(F32)
            if load:
                internal_out[rows_here, lanes] = held - forcing
                rows[slot * 6 + block][...] = forcing
                for i in range(8):
                    lines = wide_map[tile, pl.ds((block * 8 + i) * 24, 24), :]
                    row = spread_row(rows[slot * 6 + block][pl.ds(i, 1), :])
                    for d in range(3):
                        total[d] = total[d] + lines[d * 8 : d * 8 + 8] * row
        if load:
            for d in range(3):
                spread[d, here, :] = total[d]
        if weigh:
            weight[pl.ds(tile, 1), :] = jnp.sum(heavy, axis=0, keepdims=True)

    def tiles_step(step, carry):
        for slot in range(TOGETHER):
            tile_step(step * TOGETHER + slot, slot)
        return carry

    lax.fori_loop(0, TILES // TOGETHER, tiles_step, 0)
    if weigh:
        weight[...] = weight[...] * softness[...]


def send_faces(face_position, partial, near, far):
    found = [
        lookup(face_position[pl.ds(block * 8, 8), :], GRID_ROWS, lambda d, row: partial[d, pl.ds(row, 1), :], 3)
        for block in range(3)
    ]
    put_faces(found, near, far, 3)


def sum_faces(nodal, partial, face_inverse, near, far, result):
    for block in range(5):
        at = pl.ds(block * 8, 8)
        extra = face_terms(face_inverse, at, near, far, 3)
        for d in range(3):
            result[d, at, :] = nodal[d, at, :] + (partial[d, at, :] + extra[d])


def first_kernel(mass_grid, near, far, face_inverse, face_position, table, nodal, internal, wide_map,
                 stiffness, decay, misfit_grid,
                 inverse_mass, partial, near_out, far_out, internal_out,
                 scaled, corners, spread, sums, rows):
    for block in range(5):
        at = pl.ds(block * 8, 8)
        mass = mass_grid[at, :] + face_terms(face_inverse, at, near, far, 1)[0]
        inverse = 1.0 / jnp.where(table[at, :] < 0, 1.0, mass)
        inverse_mass[at, :] = inverse
        for d in range(3):
            scaled[d, at, :] = nodal[d, at, :] * inverse
    gather_corners(scaled, corners)
    element_sweep(1, True, False, wide_map, None, stiffness, decay, None, internal, corners, has_earlier_state(),
                  internal_out, spread, None, sums, rows)
    assemble(spread, misfit_grid, 1, partial)
    send_faces(face_position, partial, near_out, far_out)


def second_kernel(nodal, partial, near, far, face_inverse, face_position, inverse_mass, internal,
                  wide_map, stiffness, decay, misfit_grid,
                  nodal_grid, partial_out, near_out, far_out, internal_out,
                  scaled, corners, spread, sums, rows):
    sum_faces(nodal, partial, face_inverse, near, far, nodal_grid)
    for d in range(3):
        scaled[d] = nodal_grid[d] * inverse_mass[...]
    gather_corners(scaled, corners)
    element_sweep(0, True, False, wide_map, None, stiffness, decay, None, internal, corners, None,
                  internal_out, spread, None, sums, rows)
    assemble(spread, misfit_grid, 0, partial_out)
    send_faces(face_position, partial_out, near_out, far_out)


def finish_kernel(nodal, partial, near, far, face_inverse, nodal_grid):
    sum_faces(nodal, partial, face_inverse, near, far, nodal_grid)


def third_kernel(nodal, face_position, inverse_mass, internal, wide_map, softness, stiffness, decay, stored_in,
                 misfit_grid, nodal_grid, partial, near_out, far_out, internal_out, weight,
                 scaled, corners, spread, sums, rows, stored, arrived):
    copies = fetch((stored_in.at[1],), (stored,), arrived)
    keep = has_earlier_state()
    for d in range(3):
        value = nodal[d] * keep
        nodal_grid[d] = value
        scaled[d] = value * inverse_mass[...]
    gather_corners(scaled, corners)
    copies[0].wait()
    element_sweep(1, True, True, wide_map, softness, stiffness, decay, stored, internal, corners, keep,
                  internal_out, spread, weight, sums, rows)
    assemble(spread, misfit_grid, 1, partial)
    send_faces(face_position, partial, near_out, far_out)


def last_kernel(nodal, partial, near, far, face_inverse, inverse_mass, internal, wide_map, softness,
                stiffness, decay, stored_in, weight_in, nodal_grid, weight, scaled, corners, sums, stored, arrived):
    copies = fetch((stored_in.at[0],), (stored,), arrived)
    sum_faces(nodal, partial, face_inverse, near, far, nodal_grid)
    for d in range(3):
        scaled[d] = nodal_grid[d] * inverse_mass[...]
    gather_corners(scaled, corners)
    copies[0].wait()
    element_sweep(0, False, True, wide_map, softness, stiffness, decay, stored, internal, corners, None,
                  None, None, weight, sums, None)
    weight[...] = weight[...] + weight_in[...]


def local_kernel(inverse, nodal_grid, nodal, found_rows):
    for block in range(5):
        at = pl.ds(block * 8, 8)
        found = lookup(inverse[at, :], GRID_ROWS, lambda d, row: nodal_grid[d, pl.ds(row, 1), :], 3)
        for d in range(3):
            found_rows[d, at, :] = found[d]
    for d in range(3):
        for row in range(NODE_ROWS):
            width = min(LANES, NODES - row * LANES)
            nodal[d, :, row * LANES : row * LANES + width] = found_rows[d, pl.ds(row, 1), :width]


def shape(*dims, dtype=F32):
    return jax.ShapeDtypeStruct(dims, dtype)


def call(kernel, outs, scratch, *operands, name=None, specs=None, limit=VMEM_LIMIT):
    if specs:
        operands = [
            pltpu.with_memory_space_constraint(operand, pltpu.HBM) if spec is HBM else operand
            for operand, spec in zip(operands, specs)
        ]
    return pl.pallas_call(
        kernel,
        in_specs=specs or [VMEM] * len(operands),
        out_specs=jax.tree.map(lambda _: VMEM, outs),
        out_shape=outs,
        scratch_shapes=scratch,
        compiler_params=pltpu.CompilerParams(vmem_limit_bytes=limit),
        name=name,
    )(*operands)


NODAL = (3, ROWS, LANES)
FACES = (48, LANES)


def vm(*dims, dtype=F32):
    return pltpu.VMEM(dims, dtype)


def exchange(near, far):
    windows, count = lax.axis_size("tm"), lax.axis_size("space")
    pairs = []
    for window in range(windows):
        for place in range(count):
            other = place + 1 if place % 2 else place - 1
            own = 0 <= other < count
            pairs.append((window * count + place, window * count + other if own else (window ^ 1) * count + place))
    far = lax.ppermute(far, ("tm", "space"), pairs)
    return lax.ppermute(near, "space", [(i, i ^ 1) for i in range(count)]), far


def to_earlier(block):
    count = lax.axis_size("tm")
    return lax.ppermute(block, "tm", [((i + 1) % count, i) for i in range(count)])


def sum_windows(value):
    count = lax.axis_size("tm")
    value = value + lax.ppermute(value, "tm", [(i, i ^ 1) for i in range(count)])
    return value + lax.ppermute(value, "tm", [(i, i ^ 2) for i in range(count)])


def per_device(connect, low_face, up_face, strain_map, modulus, fluidity, element_mass, forward_strain, active, misfit,
               point_nodal, point_internal):
    modulus = modulus.reshape(TILES, LANES)
    fluidity = fluidity.reshape(TILES, LANES)
    mass = element_mass.reshape(TILES, LANES)
    nodal = to_earlier(jnp.transpose(point_nodal, (1, 0, 2)))
    internal = to_earlier(point_internal[0])
    elements = TILES * LANES
    table, inverse, face_position, mass_grid, near, far = call(
        tables_kernel,
        (shape(ROWS, LANES, dtype=I32), shape(ROWS, LANES, dtype=I32), shape(24, LANES, dtype=I32),
         shape(ROWS, LANES), shape(16, LANES), shape(16, LANES)),
        [vm(TILES * 8, LANES), vm(ROWS, LANES), vm(24, LANES, dtype=I32), vm(*connect.shape, dtype=I32),
         vm(*low_face.shape, dtype=I32), vm(*up_face.shape, dtype=I32), vm(TILES, LANES), pltpu.SemaphoreType.DMA((4,))],
        connect, low_face, up_face, mass, name="tables", specs=[HBM] * 4,
    )
    near, far = exchange(near, far)
    wide_map, stiffness, decay, softness = call(
        widen_kernel,
        (shape(TILES, STRAIN * 24, LANES), shape(STRAIN, elements), shape(2, STRAIN, elements), shape(TILES, LANES)),
        [vm(CHUNKS, STRAIN // CHUNKS, 24, elements, dtype=jnp.bfloat16), vm(TILES, LANES), vm(TILES, LANES),
         vm(*active.shape, dtype=I32), pltpu.SemaphoreType.DMA((CHUNKS,)), pltpu.SemaphoreType.DMA((3,))],
        strain_map, modulus, fluidity, active, name="widen", specs=[HBM] * 4, limit=20 * 1024 * 1024,
    )
    misfit_grid, face_inverse, nodal = call(
        loads_kernel, (shape(2, *NODAL), shape(2, ROWS, LANES, dtype=I32), shape(*NODAL)), [vm(*NODAL), vm(3, 2, NODES), pltpu.SemaphoreType.DMA((1,))],
        table, face_position, jnp.transpose(misfit, (1, 0, 2)), nodal, name="loads", specs=[VMEM, VMEM, HBM, VMEM],
    )
    work = [vm(*NODAL), vm(3, TILES * 8, LANES), vm(3, TILES * 8, LANES), [vm(72, LANES) for _ in range(6 * TOGETHER)], [vm(8, LANES) for _ in range(6 * TOGETHER)]]
    stored = [vm(STRAIN, elements, dtype=jnp.bfloat16), pltpu.SemaphoreType.DMA((1,))]
    sent = (shape(*NODAL), shape(*FACES), shape(*FACES), shape(STRAIN, elements))
    inverse_mass, partial, near, far, internal = call(
        first_kernel, (shape(ROWS, LANES),) + sent, work,
        mass_grid, near, far, face_inverse, face_position, table, nodal, internal, wide_map,
        stiffness, decay, misfit_grid, name="first",
    )
    near, far = exchange(near, far)
    nodal, partial, near, far, coarse_internal = call(
        second_kernel, (shape(*NODAL),) + sent, work,
        nodal, partial, near, far, face_inverse, face_position, inverse_mass, internal, wide_map,
        stiffness, decay, misfit_grid, name="second",
    )
    near, far = exchange(near, far)
    internal = to_earlier(coarse_internal)
    coarse = call(finish_kernel, shape(*NODAL), [], nodal, partial, near, far, face_inverse, name="finish")
    nodal = to_earlier(coarse)

    def to_local(grid):
        local = call(local_kernel, shape(3, 1, NODES), [vm(*NODAL)], inverse, grid, name="local")
        return jnp.transpose(local, (1, 0, 2))

    coarse_nodal = to_local(coarse)
    nodal, partial, near, far, fine_internal, weight = call(
        third_kernel, (shape(*NODAL),) + sent + (shape(TILES, LANES),), work + stored,
        nodal, face_position, inverse_mass, internal, wide_map, softness, stiffness, decay, forward_strain,
        misfit_grid, name="third", specs=[VMEM] * 8 + [HBM, VMEM],
    )
    near, far = exchange(near, far)
    fine, weight = call(
        last_kernel, (shape(*NODAL), shape(TILES, LANES)), [vm(*NODAL), vm(3, TILES * 8, LANES), [vm(72, LANES) for _ in range(6 * TOGETHER)]] + stored,
        nodal, partial, near, far, face_inverse, inverse_mass, fine_internal, wide_map, softness,
        stiffness, decay, forward_strain, weight, name="last", specs=[VMEM] * 11 + [HBM, VMEM],
    )
    sensitivity = sum_windows(weight)
    fine_nodal = to_local(fine)
    return coarse_nodal, coarse_internal[None], fine_nodal, fine_internal[None], sensitivity.reshape(-1)


def solution(mesh):
    in_specs = (
        P(None, "space"), P("space"), P("space"), P(None, None, "space"), P("space"), P("space"), P("space"),
        P("tm", None, "space"), P("tm", None, "space"), P("tm", None, "space"), P("tm", None, "space"),
        P("tm", None, "space"),
    )
    out_specs = (
        P("tm", None, "space"), P("tm", None, "space"), P("tm", None, "space"), P("tm", None, "space"), P("space"),
    )
    return jax.shard_map(per_device, mesh=mesh, in_specs=in_specs, out_specs=out_specs, check_vma=False)
```

```python
import jax
import jax.numpy as jnp
from jax import lax
from jax.experimental import pallas as pl
from jax.experimental.pallas import tpu as pltpu
from jax.sharding import PartitionSpec as P

LANES = 128
TILES = 24
STRAIN = 48
MAIN_ROWS = 32
GRID_ROWS = 36
ROWS = 40
NODES = 4356
NODE_ROWS = 35
FACE_ROWS = 9
VMEM_LIMIT = 12 * 1024 * 1024

VMEM = pl.BlockSpec(memory_space=pltpu.VMEM)
HBM = pl.BlockSpec(memory_space=pltpu.HBM)
F32 = jnp.float32
I32 = jnp.int32


def fetch(sources, targets, arrived):
    copies = [pltpu.make_async_copy(source, target, arrived.at[i]) for i, (source, target) in enumerate(zip(sources, targets))]
    for copy in copies:
        copy.start()
    return copies


def lane_ids():
    return lax.broadcasted_iota(I32, (8, LANES), 1)


def row_ids():
    return lax.broadcasted_iota(I32, (8, LANES), 0)


def roll(value, shift, axis):
    return pltpu.roll(value, shift % value.shape[axis], axis)


def spread_row(row):
    return jnp.broadcast_to(row, (8, LANES))


def pick(row, lanes):
    return jnp.take_along_axis(spread_row(row), lanes, axis=1)


def lookup(index, rows, row_of, count):
    high, low = index >> 7, index & 127
    found = [jnp.zeros((8, LANES), F32) for _ in range(count)]
    for row in range(rows):
        hit = high == row
        for d in range(count):
            found[d] = jnp.where(hit, pick(row_of(d, row), low), found[d])
    return found


def edge_row(at_x, at_y, at_xy):
    lane, row = lane_ids(), row_ids()
    along_x = jnp.take_along_axis(at_x, (lane & 3) * 32 + 31, axis=1)
    picked = jnp.where((row == (lane >> 2)) & (lane < 32), along_x, 0.0)
    picked = jnp.where((row == 7) & (lane >= 32) & (lane < 64), roll(at_y, -64, 1), picked)
    picked = jnp.where((row == 7) & (lane == 64), roll(at_xy, -63, 1), picked)
    return jnp.sum(picked, axis=0, keepdims=True)


def step_up_x(value):
    return jnp.where((lane_ids() & 31) == 0, 0.0, roll(value, 1, 1))


def step_up_y(value):
    turned = roll(value, 32, 1)
    below = jnp.where(row_ids() == 0, 0.0, roll(turned, 1, 0))
    return jnp.where(lane_ids() < 32, below, turned)


def assemble_plane(t00, t01, t10, t11):
    first = t00 + step_up_x(t01)
    second = t10 + step_up_x(t11)
    main = first + step_up_y(second)
    return main, edge_row(t01 + step_up_y(t11), second, t11)


def corner_planes(main, edge):
    lane, row = lane_ids(), row_ids()
    edge = spread_row(edge)
    along_x = jnp.take_along_axis(edge, row * 4 + (lane >> 5), axis=1)
    moved_x = jnp.where((lane & 31) == 31, along_x, roll(main, -1, 1))

    def move_y(value, last):
        turned = roll(value, -32, 1)
        above = jnp.where(row == 7, last, roll(turned, -1, 0))
        return jnp.where(lane < 96, turned, above)

    return main, moved_x, move_y(main, roll(edge, 64, 1)), move_y(moved_x, roll(edge, 63, 1))


def even_place():
    return lax.axis_index("space") % 2 == 0


def has_earlier_state():
    return jnp.where(lax.axis_index("tm") < lax.axis_size("tm") - 1, 1.0, 0.0)


def has_far_face():
    place = lax.axis_index("space")
    return jnp.where((place > 0) & (place < lax.axis_size("space") - 1), 1.0, 0.0)


def tables_kernel(connect_in, low_in, up_in, mass_in, table, inverse, face_position, mass_grid, mass_near, mass_far,
                  flat, numbers, faces, connect, low_face, up_face, mass, arrived):
    copies = fetch((connect_in, low_in, up_in, mass_in), (connect, low_face, up_face, mass), arrived)
    even = even_place()
    faces[...] = jnp.full((24, LANES), -1, I32)
    for copy in copies:
        copy.wait()
    for row in range(FACE_ROWS):
        width = min(LANES, low_face.shape[0] - row * LANES)
        at = slice(row * LANES, row * LANES + width)
        low, up = low_face[at], up_face[at]
        near, far = jnp.where(even, up, low), jnp.where(even, low, up)
        to = (row, row + 8) if row < 8 else (16, 17)
        faces[to[0], :width] = near
        faces[to[1], :width] = far
    for tile in range(TILES):
        flat[pl.ds(tile * 8, 8), :] = connect[:, tile * LANES : (tile + 1) * LANES].astype(F32)
    for plane in range(4):
        base, shift = (plane, 0) if plane < 3 else (2, 4)

        def corner(c):
            return flat[pl.ds(base * 64 + shift + c, 8, stride=8), :]

        numbers[pl.ds(plane * 8, 8), :] = corner(0)
        numbers[pl.ds(MAIN_ROWS + plane, 1), :] = edge_row(corner(1), corner(2), corner(3))
        below = mass[pl.ds((plane - 1) * 8, 8), :] if plane > 0 else 0.0
        above = mass[pl.ds(plane * 8, 8), :] if plane < 3 else 0.0
        both = (below + above) / 8.0
        main, edge = assemble_plane(both, both, both, both)
        mass_grid[pl.ds(plane * 8, 8), :] = main
        mass_grid[pl.ds(MAIN_ROWS + plane, 1), :] = edge
    numbers[pl.ds(GRID_ROWS, 4), :] = jnp.full((4, LANES), -1.0, F32)
    mass_grid[pl.ds(GRID_ROWS, 4), :] = jnp.zeros((4, LANES), F32)
    edges = numbers[pl.ds(MAIN_ROWS, 8), :]
    numbers[pl.ds(MAIN_ROWS, 8), :] = jnp.where((lane_ids() > 64) | (row_ids() > 3), -1.0, edges)
    table[...] = numbers[...].astype(I32)

    rows_at = lax.broadcasted_iota(I32, (ROWS, LANES), 0)
    lanes_at = lax.broadcasted_iota(I32, (LANES, LANES), 0)
    own_lane = lax.broadcasted_iota(I32, (ROWS, LANES), 1).astype(F32)
    found = jnp.zeros((2 * ROWS, LANES), F32)
    for row in range(GRID_ROWS):
        index = table[pl.ds(row, 1), :]
        hit = jnp.broadcast_to(index >> 7, (ROWS, LANES)) == rows_at
        left = jnp.concatenate([jnp.where(hit, float(row), 0.0), jnp.where(hit, own_lane, 0.0)], axis=0)
        right = jnp.where(jnp.broadcast_to(index & 127, (LANES, LANES)) == lanes_at, 1.0, 0.0)
        found = found + lax.dot_general(
            left.astype(jnp.bfloat16), right.astype(jnp.bfloat16), (((1,), (1,)), ((), ())), preferred_element_type=F32
        )
    numbers[...] = found[:ROWS] * 128.0 + found[ROWS:]
    inverse[...] = numbers[...].astype(I32)

    found = []
    for block in range(3):
        at = pl.ds(block * 8, 8)
        local = faces[at, :]
        position = lookup(local, NODE_ROWS, lambda d, row: numbers[pl.ds(row, 1), :], 1)[0]
        position = jnp.where(local < 0, -1, position.astype(I32))
        face_position[at, :] = position
        found.append(lookup(position, GRID_ROWS, lambda d, row: mass_grid[pl.ds(row, 1), :], 1))
    put_faces(found, mass_near, mass_far, 1)


def put_faces(found, near, far, count):
    for d in range(count):
        near[pl.ds(d * 16, 8), :] = found[0][d]
        near[pl.ds(d * 16 + 8, 8), :] = found[2][d]
        far[pl.ds(d * 16, 8), :] = found[1][d]
        far[pl.ds(d * 16 + 8, 8), :] = roll(found[2][d], -1, 0)


def local_to_grid(source, local, rows, table, put):
    for d in range(3):
        source[d, pl.ds(32, 8), :] = jnp.zeros((8, LANES), F32)
        for row in range(NODE_ROWS):
            width = min(LANES, NODES - row * LANES)
            source[d, pl.ds(row, 1), :width] = local[d, rows, row * LANES : row * LANES + width]
    for block in range(5):
        at = pl.ds(block * 8, 8)
        put(at, lookup(table[at, :], NODE_ROWS, lambda d, row: source[d, pl.ds(row, 1), :], 3))


def loads_kernel(table, face_position, misfit_in, nodal, misfit_grid, face_inverse, nodal_grid, source, misfit, arrived):
    copies = fetch((misfit_in,), (misfit,), arrived)
    keep = has_earlier_state()

    def put_nodal(at, found):
        for d in range(3):
            nodal_grid[d, at, :] = found[d] * keep

    local_to_grid(source, nodal, pl.ds(0, 1), table, put_nodal)
    copies[0].wait()
    for section in range(2):

        def put(at, found):
            for d in range(3):
                misfit_grid[section, d, at, :] = found[d]

        local_to_grid(source, misfit, pl.ds(section, 1), table, put)
    rows_at = lax.broadcasted_iota(I32, (ROWS, LANES), 0)
    lanes_at = lax.broadcasted_iota(I32, (LANES, LANES), 0)
    own_lane = lax.broadcasted_iota(I32, (ROWS, LANES), 1).astype(F32)
    for side in range(2):
        found = jnp.zeros((2 * ROWS, LANES), F32)
        for row in range(FACE_ROWS):
            index = face_position[pl.ds(row + side * 8 if row < 8 else 16 + side, 1), :]
            hit = jnp.broadcast_to(index >> 7, (ROWS, LANES)) == rows_at
            left = jnp.concatenate([jnp.where(hit, float(row + 1), 0.0), jnp.where(hit, own_lane, 0.0)], axis=0)
            right = jnp.where(jnp.broadcast_to(index & 127, (LANES, LANES)) == lanes_at, 1.0, 0.0)
            found = found + lax.dot_general(
                left.astype(jnp.bfloat16), right.astype(jnp.bfloat16), (((1,), (1,)), ((), ())), preferred_element_type=F32
            )
        face_inverse[side] = ((found[:ROWS] - 1.0) * 128.0 + found[ROWS:]).astype(I32)


CHUNKS = 6


def widen_kernel(strain_map, modulus_in, fluidity_in, active_in, wide_map, stiffness, decay, softness,
                 narrow, modulus, fluidity, active, arrived, small_arrived):
    depth = STRAIN // CHUNKS
    small = fetch((modulus_in, fluidity_in, active_in), (modulus, fluidity, active), small_arrived)
    copies = fetch(
        [strain_map.at[pl.ds(part * depth, depth)] for part in range(CHUNKS)], [narrow.at[part] for part in range(CHUNKS)], arrived
    )
    for copy in small:
        copy.wait()
    softness[...] = 1.0 / modulus[...]

    def tile_step(tile, carry):
        lanes = pl.ds(pl.multiple_of(tile * LANES, LANES), LANES)
        own = spread_row(modulus[pl.ds(tile, 1), :])
        rates = [active[n, :, lanes].astype(F32) * fluidity[pl.ds(tile, 1), :] for n in range(2)]
        for block in range(6):
            row = row_ids() + block * 8
            here = jnp.where(row % 6 < 3, 2.0, 1.0) * own
            stiffness[pl.ds(block * 8, 8), lanes] = here
            point = block * 8 // 6
            for n in range(2):
                rate = jnp.where(row < (point + 1) * 6, rates[n][point : point + 1], rates[n][point + 1 : point + 2])
                decay[n, pl.ds(block * 8, 8), lanes] = here * rate
        return carry

    lax.fori_loop(0, TILES, tile_step, 0)
    for part in range(CHUNKS):
        copies[part].wait()

        def row_step(row, carry):
            to = pl.ds(pl.multiple_of((part * depth + row) * 24, 8), 24)
            for tile in range(TILES):
                wide_map[tile, to, :] = narrow[part, row, :, tile * LANES : (tile + 1) * LANES].astype(F32)
            return carry

        lax.fori_loop(0, depth, row_step, 0)


def face_terms(face_inverse, at, near, far, count):
    from_near = lookup(face_inverse[0, at, :], FACE_ROWS, lambda d, row: near[pl.ds(d * 16 + row, 1), :], count)
    from_far = lookup(face_inverse[1, at, :], FACE_ROWS, lambda d, row: far[pl.ds(d * 16 + row, 1), :], count)
    keep = has_far_face()
    return [from_near[d] + from_far[d] * keep for d in range(count)]


def gather_corners(scaled, corners):
    for d in range(3):
        for plane in range(4):
            shifted = corner_planes(scaled[d, pl.ds(plane * 8, 8), :], scaled[d, pl.ds(MAIN_ROWS + plane, 1), :])
            for up in range(2):
                layer = plane - up
                if 0 <= layer < 3:
                    for c in range(4):
                        corners[d, pl.ds(layer * 64 + up * 4 + c, 8, stride=8), :] = shifted[c]


def assemble(spread, misfit_grid, section, partial):
    for d in range(3):
        edges = []
        for plane in range(4):
            terms = []
            for c in range(4):
                total = None
                for up in range(2):
                    layer = plane - up
                    if 0 <= layer < 3:
                        term = spread[d, pl.ds(layer * 64 + up * 4 + c, 8, stride=8), :]
                        total = term if total is None else total + term
                terms.append(total)
            main, edge = assemble_plane(*terms)
            at = pl.ds(plane * 8, 8)
            partial[d, at, :] = main + misfit_grid[section, d, at, :]
            edges.append(edge)
        at = pl.ds(MAIN_ROWS, 8)
        edges = jnp.concatenate(edges + [jnp.zeros((4, LANES), F32)], axis=0)
        partial[d, at, :] = edges + misfit_grid[section, d, at, :]


PITCH = 9
TOGETHER = 2


def element_sweep(section, load, weigh, wide_map, softness, stiffness, decay, stored, internal, corners,
                  keep, internal_out, spread, weight, sums, rows):
    def tile_step(tile, slot):
        lanes = pl.ds(pl.multiple_of(tile * LANES, LANES), LANES)
        here = pl.ds(pl.multiple_of(tile * 8, 8), 8)
        scaled = [corners[d, here, :] for d in range(3)]
        total = [jnp.zeros((8, LANES), F32) for _ in range(3)]
        heavy = jnp.zeros((8, LANES), F32)
        for block in range(6):
            for i in range(8):
                lines = wide_map[tile, pl.ds((block * 8 + i) * 24, 24), :]
                sums[slot * 6 + block][pl.ds(i * PITCH, 8), :] = (
                    lines[0:8] * scaled[0] + lines[8:16] * scaled[1] + lines[16:24] * scaled[2]
                )
            product = sums[slot * 6 + block][pl.ds(0, 8, stride=PITCH), :]
            for i in range(1, 8):
                product = product + sums[slot * 6 + block][pl.ds(i, 8, stride=PITCH), :]
            rows_here = pl.ds(block * 8, 8)
            held = internal[rows_here, lanes]
            if keep is not None:
                held = held * keep
            forcing = decay[section, rows_here, lanes] * held - stiffness[rows_here, lanes] * product
            if weigh:
                heavy = heavy + forcing * stored[rows_here, lanes].astype(F32)
            if load:
                internal_out[rows_here, lanes] = held - forcing
                rows[slot * 6 + block][...] = forcing
                for i in range(8):
                    lines = wide_map[tile, pl.ds((block * 8 + i) * 24, 24), :]
                    row = spread_row(rows[slot * 6 + block][pl.ds(i, 1), :])
                    for d in range(3):
                        total[d] = total[d] + lines[d * 8 : d * 8 + 8] * row
        if load:
            for d in range(3):
                spread[d, here, :] = total[d]
        if weigh:
            weight[pl.ds(tile, 1), :] = jnp.sum(heavy, axis=0, keepdims=True)

    def tiles_step(step, carry):
        for slot in range(TOGETHER):
            tile_step(step * TOGETHER + slot, slot)
        return carry

    lax.fori_loop(0, TILES // TOGETHER, tiles_step, 0)
    if weigh:
        weight[...] = weight[...] * softness[...]


def send_faces(face_position, partial, near, far):
    found = [
        lookup(face_position[pl.ds(block * 8, 8), :], GRID_ROWS, lambda d, row: partial[d, pl.ds(row, 1), :], 3)
        for block in range(3)
    ]
    put_faces(found, near, far, 3)


def sum_faces(own, face_inverse, near, far, put):
    for block in range(5):
        at = pl.ds(block * 8, 8)
        extra = face_terms(face_inverse, at, near, far, 3)
        for d in range(3):
            put(d, at, own[d, at, :] + extra[d])


def send_step(nodal, spread, misfit_grid, section, face_position, partial, own, near, far):
    assemble(spread, misfit_grid, section, partial)
    for d in range(3):
        own[d] = nodal[d] + partial[d]
    send_faces(face_position, partial, near, far)


def first_kernel(mass_grid, near, far, face_inverse, face_position, table, nodal, internal, wide_map,
                 stiffness, decay, misfit_grid,
                 inverse_mass, own, near_out, far_out, internal_out,
                 partial, scaled, corners, spread, sums, rows):
    for block in range(5):
        at = pl.ds(block * 8, 8)
        mass = mass_grid[at, :] + face_terms(face_inverse, at, near, far, 1)[0]
        inverse = 1.0 / jnp.where(table[at, :] < 0, 1.0, mass)
        inverse_mass[at, :] = inverse
        for d in range(3):
            scaled[d, at, :] = nodal[d, at, :] * inverse
    gather_corners(scaled, corners)
    element_sweep(1, True, False, wide_map, None, stiffness, decay, None, internal, corners, has_earlier_state(),
                  internal_out, spread, None, sums, rows)
    send_step(nodal, spread, misfit_grid, 1, face_position, partial, own, near_out, far_out)


def second_kernel(own_in, near, far, face_inverse, face_position, inverse_mass, internal,
                  wide_map, stiffness, decay, misfit_grid, stored_in,
                  own, near_out, far_out, internal_out, stored,
                  partial, scaled, corners, spread, sums, rows, nodal, arrived):
    copies = fetch((stored_in,), (stored,), arrived)

    def put(d, at, value):
        nodal[d, at, :] = value
        scaled[d, at, :] = value * inverse_mass[at, :]

    sum_faces(own_in, face_inverse, near, far, put)
    gather_corners(scaled, corners)
    element_sweep(0, True, False, wide_map, None, stiffness, decay, None, internal, corners, None,
                  internal_out, spread, None, sums, rows)
    send_step(nodal, spread, misfit_grid, 0, face_position, partial, own, near_out, far_out)
    copies[0].wait()


def third_kernel(own_in, near, far, face_inverse, face_position, inverse_mass, internal, wide_map, softness, stiffness,
                 decay, stored, misfit_grid, coarse_internal,
                 coarse, own, near_out, far_out, internal_out, weight, coarse_internal_out,
                 partial, scaled, corners, spread, sums, rows, nodal, arrived):
    copies = fetch((coarse_internal,), (coarse_internal_out,), arrived)
    keep = has_earlier_state()

    def put(d, at, value):
        coarse[d, at, :] = value
        nodal[d, at, :] = value * keep
        scaled[d, at, :] = value * (inverse_mass[at, :] * keep)

    sum_faces(own_in, face_inverse, near, far, put)
    gather_corners(scaled, corners)
    element_sweep(1, True, True, wide_map, softness, stiffness, decay, stored.at[1], internal, corners, keep,
                  internal_out, spread, weight, sums, rows)
    send_step(nodal, spread, misfit_grid, 1, face_position, partial, own, near_out, far_out)
    copies[0].wait()


def last_kernel(own, near, far, face_inverse, inverse_mass, internal, wide_map, softness,
                stiffness, decay, stored, weight_in, coarse, fine, weight, fine_internal, scaled, corners, sums, arrived):
    copies = fetch((internal,), (fine_internal,), arrived)

    def put(d, at, value):
        fine[d, at, :] = value
        scaled[d, at, :] = value * inverse_mass[at, :]

    sum_faces(own, face_inverse, near, far, put)
    gather_corners(scaled, corners)
    element_sweep(0, False, True, wide_map, softness, stiffness, decay, stored.at[0], internal, corners, None,
                  None, None, weight, sums, None)
    weight[...] = weight[...] + weight_in[...]
    copies[0].wait()


def local_kernel(inverse, coarse, fine, coarse_nodal, fine_nodal, found_rows):
    for grid, nodal in ((coarse, coarse_nodal), (fine, fine_nodal)):
        for block in range(5):
            at = pl.ds(block * 8, 8)
            found = lookup(inverse[at, :], GRID_ROWS, lambda d, row: grid[d, pl.ds(row, 1), :], 3)
            for d in range(3):
                found_rows[d, at, :] = found[d]
        for d in range(3):
            for row in range(NODE_ROWS):
                width = min(LANES, NODES - row * LANES)
                nodal[d, :, row * LANES : row * LANES + width] = found_rows[d, pl.ds(row, 1), :width]


def shape(*dims, dtype=F32):
    return jax.ShapeDtypeStruct(dims, dtype)


def call(kernel, outs, scratch, *operands, name=None, specs=None, limit=VMEM_LIMIT, to_hbm=()):
    if specs:
        operands = [
            pltpu.with_memory_space_constraint(operand, pltpu.HBM) if spec is HBM else operand
            for operand, spec in zip(operands, specs)
        ]
    return pl.pallas_call(
        kernel,
        in_specs=specs or [VMEM] * len(operands),
        out_specs=[HBM if i in to_hbm else VMEM for i in range(len(outs))] if isinstance(outs, tuple) else VMEM,
        out_shape=outs,
        scratch_shapes=scratch,
        compiler_params=pltpu.CompilerParams(vmem_limit_bytes=limit),
        name=name,
    )(*operands)


NODAL = (3, ROWS, LANES)
FACES = (48, LANES)


def vm(*dims, dtype=F32):
    return pltpu.VMEM(dims, dtype)


def exchange(near, far, back=0):
    windows, count = lax.axis_size("tm"), lax.axis_size("space")
    near_pairs, far_pairs = [], []
    for window in range(windows):
        for place in range(count):
            source, target = window * count + place, (window - back) % windows * count
            near_pairs.append((source, target + (place ^ 1)))
            other = place + 1 if place % 2 else place - 1
            if not 0 <= other < count:
                other, target = place, target if back else (window ^ 1) * count
            far_pairs.append((source, target + other))
    axes = ("tm", "space")
    far = lax.ppermute(far, axes, far_pairs)
    return lax.ppermute(near, axes, near_pairs), far


def to_earlier(block):
    count = lax.axis_size("tm")
    return lax.ppermute(block, "tm", [((i + 1) % count, i) for i in range(count)])


def to_later(block):
    count = lax.axis_size("tm")
    return lax.ppermute(block, "tm", [(i, (i + 1) % count) for i in range(count)])


def sum_windows(value):
    count = lax.axis_size("tm")
    value = value + lax.ppermute(value, "tm", [(i, i ^ 1) for i in range(count)])
    return value + lax.ppermute(value, "tm", [(i, i ^ 2) for i in range(count)])


def per_device(connect, low_face, up_face, strain_map, modulus, fluidity, element_mass, forward_strain, active, misfit,
               point_nodal, point_internal):
    modulus = modulus.reshape(TILES, LANES)
    fluidity = fluidity.reshape(TILES, LANES)
    mass = element_mass.reshape(TILES, LANES)
    nodal = to_earlier(jnp.transpose(point_nodal, (1, 0, 2)))
    internal = to_earlier(point_internal[0])
    elements = TILES * LANES
    table, inverse, face_position, mass_grid, near, far = call(
        tables_kernel,
        (shape(ROWS, LANES, dtype=I32), shape(ROWS, LANES, dtype=I32), shape(24, LANES, dtype=I32),
         shape(ROWS, LANES), shape(16, LANES), shape(16, LANES)),
        [vm(TILES * 8, LANES), vm(ROWS, LANES), vm(24, LANES, dtype=I32), vm(*connect.shape, dtype=I32),
         vm(*low_face.shape, dtype=I32), vm(*up_face.shape, dtype=I32), vm(TILES, LANES), pltpu.SemaphoreType.DMA((4,))],
        connect, low_face, up_face, mass, name="tables", specs=[HBM] * 4,
    )
    near, far = exchange(near, far)
    wide_map, stiffness, decay, softness = call(
        widen_kernel,
        (shape(TILES, STRAIN * 24, LANES), shape(STRAIN, elements), shape(2, STRAIN, elements), shape(TILES, LANES)),
        [vm(CHUNKS, STRAIN // CHUNKS, 24, elements, dtype=jnp.bfloat16), vm(TILES, LANES), vm(TILES, LANES),
         vm(*active.shape, dtype=I32), pltpu.SemaphoreType.DMA((CHUNKS,)), pltpu.SemaphoreType.DMA((3,))],
        strain_map, modulus, fluidity, active, name="widen", specs=[HBM] * 4, limit=20 * 1024 * 1024,
    )
    misfit_grid, face_inverse, nodal = call(
        loads_kernel, (shape(2, *NODAL), shape(2, ROWS, LANES, dtype=I32), shape(*NODAL)), [vm(*NODAL), vm(3, 2, NODES), pltpu.SemaphoreType.DMA((1,))],
        table, face_position, jnp.transpose(misfit, (1, 0, 2)), nodal, name="loads", specs=[VMEM, VMEM, HBM, VMEM],
    )
    sums = [vm(72, LANES) for _ in range(6 * TOGETHER)]
    work = [vm(*NODAL), vm(*NODAL), vm(3, TILES * 8, LANES), vm(3, TILES * 8, LANES), sums,
            [vm(8, LANES) for _ in range(6 * TOGETHER)]]
    more = [vm(*NODAL), pltpu.SemaphoreType.DMA((1,))]
    sent = (shape(*NODAL), shape(*FACES), shape(*FACES), shape(STRAIN, elements))
    inverse_mass, own, near, far, internal = call(
        first_kernel, (shape(ROWS, LANES),) + sent, work,
        mass_grid, near, far, face_inverse, face_position, table, nodal, internal, wide_map,
        stiffness, decay, misfit_grid, name="first",
    )
    near, far = exchange(near, far)
    own, near, far, internal, stored = call(
        second_kernel, sent + (shape(*forward_strain.shape, dtype=jnp.bfloat16),), work + more,
        own, near, far, face_inverse, face_position, inverse_mass, internal, wide_map,
        stiffness, decay, misfit_grid, forward_strain, name="second", specs=[VMEM] * 11 + [HBM],
    )
    earlier = to_earlier(internal)
    near, far = exchange(near, far, 1)
    own = to_earlier(own)

    coarse, own, near, far, held, weight, coarse_internal = call(
        third_kernel, (shape(*NODAL),) + sent + (shape(TILES, LANES), shape(STRAIN, elements)), work + more,
        own, near, far, face_inverse, face_position, inverse_mass, earlier, wide_map, softness, stiffness, decay, stored,
        misfit_grid, internal, name="third", to_hbm=(6,),
    )
    near, far = exchange(near, far)
    coarse = to_later(coarse)
    fine, weight, fine_internal = call(
        last_kernel, (shape(*NODAL), shape(TILES, LANES), shape(STRAIN, elements)),
        [vm(*NODAL), vm(3, TILES * 8, LANES), sums, pltpu.SemaphoreType.DMA((1,))],
        own, near, far, face_inverse, inverse_mass, held, wide_map, softness,
        stiffness, decay, stored, weight, coarse, name="last", to_hbm=(2,),
    )
    sensitivity = sum_windows(weight)
    coarse_nodal, fine_nodal = call(
        local_kernel, (shape(3, 1, NODES), shape(3, 1, NODES)), [vm(*NODAL)], inverse, coarse, fine, name="local"
    )
    coarse_nodal, fine_nodal = jnp.transpose(coarse_nodal, (1, 0, 2)), jnp.transpose(fine_nodal, (1, 0, 2))
    return coarse_nodal, coarse_internal[None], fine_nodal, fine_internal[None], sensitivity.reshape(-1)


def solution(mesh):
    in_specs = (
        P(None, "space"), P("space"), P("space"), P(None, None, "space"), P("space"), P("space"), P("space"),
        P("tm", None, "space"), P("tm", None, "space"), P("tm", None, "space"), P("tm", None, "space"),
        P("tm", None, "space"),
    )
    out_specs = (
        P("tm", None, "space"), P("tm", None, "space"), P("tm", None, "space"), P("tm", None, "space"), P("space"),
    )
    return jax.shard_map(per_device, mesh=mesh, in_specs=in_specs, out_specs=out_specs, check_vma=False)
```

```python
import jax
import jax.numpy as jnp
from jax import lax
from jax.experimental import pallas as pl
from jax.experimental.pallas import tpu as pltpu
from jax.sharding import PartitionSpec as P

LANES = 128
TILES = 24
STRAIN = 48
MAIN_ROWS = 32
GRID_ROWS = 36
ROWS = 40
NODES = 4356
NODE_ROWS = 35
FACE_ROWS = 9
VMEM_LIMIT = 12 * 1024 * 1024

VMEM = pl.BlockSpec(memory_space=pltpu.VMEM)
HBM = pl.BlockSpec(memory_space=pltpu.HBM)
F32 = jnp.float32
I32 = jnp.int32


def fetch(sources, targets, arrived):
    copies = [pltpu.make_async_copy(source, target, arrived.at[i]) for i, (source, target) in enumerate(zip(sources, targets))]
    for copy in copies:
        copy.start()
    return copies


def lane_ids():
    return lax.broadcasted_iota(I32, (8, LANES), 1)


def row_ids():
    return lax.broadcasted_iota(I32, (8, LANES), 0)


def roll(value, shift, axis):
    return pltpu.roll(value, shift % value.shape[axis], axis)


def spread_row(row):
    return jnp.broadcast_to(row, (8, LANES))


def pick(row, lanes):
    return jnp.take_along_axis(spread_row(row), lanes, axis=1)


def lookup(index, rows, row_of, count):
    high, low = index >> 7, index & 127
    found = [jnp.zeros((8, LANES), F32) for _ in range(count)]
    for row in range(rows):
        hit = high == row
        for d in range(count):
            found[d] = jnp.where(hit, pick(row_of(d, row), low), found[d])
    return found


def edge_row(at_x, at_y, at_xy):
    lane, row = lane_ids(), row_ids()
    along_x = jnp.take_along_axis(at_x, (lane & 3) * 32 + 31, axis=1)
    picked = jnp.where((row == (lane >> 2)) & (lane < 32), along_x, 0.0)
    picked = jnp.where((row == 7) & (lane >= 32) & (lane < 64), roll(at_y, -64, 1), picked)
    picked = jnp.where((row == 7) & (lane == 64), roll(at_xy, -63, 1), picked)
    return jnp.sum(picked, axis=0, keepdims=True)


def step_up_x(value):
    return jnp.where((lane_ids() & 31) == 0, 0.0, roll(value, 1, 1))


def step_up_y(value):
    turned = roll(value, 32, 1)
    below = jnp.where(row_ids() == 0, 0.0, roll(turned, 1, 0))
    return jnp.where(lane_ids() < 32, below, turned)


def assemble_plane(t00, t01, t10, t11):
    first = t00 + step_up_x(t01)
    second = t10 + step_up_x(t11)
    main = first + step_up_y(second)
    return main, edge_row(t01 + step_up_y(t11), second, t11)


def corner_planes(main, edge):
    lane, row = lane_ids(), row_ids()
    edge = spread_row(edge)
    along_x = jnp.take_along_axis(edge, row * 4 + (lane >> 5), axis=1)
    moved_x = jnp.where((lane & 31) == 31, along_x, roll(main, -1, 1))

    def move_y(value, last):
        turned = roll(value, -32, 1)
        above = jnp.where(row == 7, last, roll(turned, -1, 0))
        return jnp.where(lane < 96, turned, above)

    return main, moved_x, move_y(main, roll(edge, 64, 1)), move_y(moved_x, roll(edge, 63, 1))


def even_place():
    return lax.axis_index("space") % 2 == 0


def has_earlier_state():
    return jnp.where(lax.axis_index("tm") < lax.axis_size("tm") - 1, 1.0, 0.0)


def has_far_face():
    place = lax.axis_index("space")
    return jnp.where((place > 0) & (place < lax.axis_size("space") - 1), 1.0, 0.0)


def tables_kernel(connect_in, low_in, up_in, mass_in, table, inverse, face_position, mass_grid, mass_near, mass_far,
                  flat, numbers, faces, connect, low_face, up_face, mass, arrived):
    copies = fetch((connect_in, low_in, up_in, mass_in), (connect, low_face, up_face, mass), arrived)
    even = even_place()
    faces[...] = jnp.full((24, LANES), -1, I32)
    for copy in copies:
        copy.wait()
    for row in range(FACE_ROWS):
        width = min(LANES, low_face.shape[0] - row * LANES)
        at = slice(row * LANES, row * LANES + width)
        low, up = low_face[at], up_face[at]
        near, far = jnp.where(even, up, low), jnp.where(even, low, up)
        to = (row, row + 8) if row < 8 else (16, 17)
        faces[to[0], :width] = near
        faces[to[1], :width] = far
    for tile in range(TILES):
        flat[pl.ds(tile * 8, 8), :] = connect[:, tile * LANES : (tile + 1) * LANES].astype(F32)
    for plane in range(4):
        base, shift = (plane, 0) if plane < 3 else (2, 4)

        def corner(c):
            return flat[pl.ds(base * 64 + shift + c, 8, stride=8), :]

        numbers[pl.ds(plane * 8, 8), :] = corner(0)
        numbers[pl.ds(MAIN_ROWS + plane, 1), :] = edge_row(corner(1), corner(2), corner(3))
        below = mass[pl.ds((plane - 1) * 8, 8), :] if plane > 0 else 0.0
        above = mass[pl.ds(plane * 8, 8), :] if plane < 3 else 0.0
        both = (below + above) / 8.0
        main, edge = assemble_plane(both, both, both, both)
        mass_grid[pl.ds(plane * 8, 8), :] = main
        mass_grid[pl.ds(MAIN_ROWS + plane, 1), :] = edge
    numbers[pl.ds(GRID_ROWS, 4), :] = jnp.full((4, LANES), -1.0, F32)
    mass_grid[pl.ds(GRID_ROWS, 4), :] = jnp.zeros((4, LANES), F32)
    edges = numbers[pl.ds(MAIN_ROWS, 8), :]
    numbers[pl.ds(MAIN_ROWS, 8), :] = jnp.where((lane_ids() > 64) | (row_ids() > 3), -1.0, edges)
    table[...] = numbers[...].astype(I32)

    rows_at = lax.broadcasted_iota(I32, (ROWS, LANES), 0)
    lanes_at = lax.broadcasted_iota(I32, (LANES, LANES), 0)
    own_lane = lax.broadcasted_iota(I32, (ROWS, LANES), 1).astype(F32)
    found = jnp.zeros((2 * ROWS, LANES), F32)
    for row in range(GRID_ROWS):
        index = table[pl.ds(row, 1), :]
        hit = jnp.broadcast_to(index >> 7, (ROWS, LANES)) == rows_at
        left = jnp.concatenate([jnp.where(hit, float(row), 0.0), jnp.where(hit, own_lane, 0.0)], axis=0)
        right = jnp.where(jnp.broadcast_to(index & 127, (LANES, LANES)) == lanes_at, 1.0, 0.0)
        found = found + lax.dot_general(
            left.astype(jnp.bfloat16), right.astype(jnp.bfloat16), (((1,), (1,)), ((), ())), preferred_element_type=F32
        )
    numbers[...] = found[:ROWS] * 128.0 + found[ROWS:]
    inverse[...] = numbers[...].astype(I32)

    found = []
    for block in range(3):
        at = pl.ds(block * 8, 8)
        local = faces[at, :]
        position = lookup(local, NODE_ROWS, lambda d, row: numbers[pl.ds(row, 1), :], 1)[0]
        position = jnp.where(local < 0, -1, position.astype(I32))
        face_position[at, :] = position
        found.append(lookup(position, GRID_ROWS, lambda d, row: mass_grid[pl.ds(row, 1), :], 1))
    put_faces(found, mass_near, mass_far, 1)


def put_faces(found, near, far, count):
    for d in range(count):
        near[pl.ds(d * 16, 8), :] = found[0][d]
        near[pl.ds(d * 16 + 8, 8), :] = found[2][d]
        far[pl.ds(d * 16, 8), :] = found[1][d]
        far[pl.ds(d * 16 + 8, 8), :] = roll(found[2][d], -1, 0)


def local_to_grid(source, local, rows, table, put):
    for d in range(3):
        source[d, pl.ds(32, 8), :] = jnp.zeros((8, LANES), F32)
        for row in range(NODE_ROWS):
            width = min(LANES, NODES - row * LANES)
            source[d, pl.ds(row, 1), :width] = local[d, rows, row * LANES : row * LANES + width]
    for block in range(5):
        at = pl.ds(block * 8, 8)
        put(at, lookup(table[at, :], NODE_ROWS, lambda d, row: source[d, pl.ds(row, 1), :], 3))


def loads_kernel(table, face_position, misfit_in, nodal, misfit_grid, face_inverse, nodal_grid, source, misfit, arrived):
    copies = fetch((misfit_in,), (misfit,), arrived)
    keep = has_earlier_state()

    def put_nodal(at, found):
        for d in range(3):
            nodal_grid[d, at, :] = found[d] * keep

    local_to_grid(source, nodal, pl.ds(0, 1), table, put_nodal)
    copies[0].wait()
    for section in range(2):

        def put(at, found):
            for d in range(3):
                misfit_grid[section, d, at, :] = found[d]

        local_to_grid(source, misfit, pl.ds(section, 1), table, put)
    rows_at = lax.broadcasted_iota(I32, (ROWS, LANES), 0)
    lanes_at = lax.broadcasted_iota(I32, (LANES, LANES), 0)
    own_lane = lax.broadcasted_iota(I32, (ROWS, LANES), 1).astype(F32)
    for side in range(2):
        found = jnp.zeros((2 * ROWS, LANES), F32)
        for row in range(FACE_ROWS):
            index = face_position[pl.ds(row + side * 8 if row < 8 else 16 + side, 1), :]
            hit = jnp.broadcast_to(index >> 7, (ROWS, LANES)) == rows_at
            left = jnp.concatenate([jnp.where(hit, float(row + 1), 0.0), jnp.where(hit, own_lane, 0.0)], axis=0)
            right = jnp.where(jnp.broadcast_to(index & 127, (LANES, LANES)) == lanes_at, 1.0, 0.0)
            found = found + lax.dot_general(
                left.astype(jnp.bfloat16), right.astype(jnp.bfloat16), (((1,), (1,)), ((), ())), preferred_element_type=F32
            )
        face_inverse[side] = ((found[:ROWS] - 1.0) * 128.0 + found[ROWS:]).astype(I32)


CHUNKS = 6


def widen_kernel(strain_map, modulus_in, fluidity_in, active_in, wide_map, stiffness, decay, softness,
                 narrow, modulus, fluidity, active, arrived, small_arrived):
    depth = STRAIN // CHUNKS
    small = fetch((modulus_in, fluidity_in, active_in), (modulus, fluidity, active), small_arrived)
    copies = fetch(
        [strain_map.at[pl.ds(part * depth, depth)] for part in range(CHUNKS)], [narrow.at[part] for part in range(CHUNKS)], arrived
    )
    for copy in small:
        copy.wait()
    softness[...] = 1.0 / modulus[...]

    def tile_step(tile, carry):
        lanes = pl.ds(pl.multiple_of(tile * LANES, LANES), LANES)
        own = spread_row(modulus[pl.ds(tile, 1), :])
        rates = [active[n, :, lanes].astype(F32) * fluidity[pl.ds(tile, 1), :] for n in range(2)]
        for block in range(6):
            row = row_ids() + block * 8
            here = jnp.where(row % 6 < 3, 2.0, 1.0) * own
            stiffness[pl.ds(block * 8, 8), lanes] = here
            point = block * 8 // 6
            for n in range(2):
                rate = jnp.where(row < (point + 1) * 6, rates[n][point : point + 1], rates[n][point + 1 : point + 2])
                decay[n, pl.ds(block * 8, 8), lanes] = here * rate
        return carry

    lax.fori_loop(0, TILES, tile_step, 0)
    for part in range(CHUNKS):
        copies[part].wait()

        def row_step(row, carry):
            to = pl.ds(pl.multiple_of((part * depth + row) * 24, 8), 24)
            for tile in range(TILES):
                wide_map[tile, to, :] = narrow[part, row, :, tile * LANES : (tile + 1) * LANES].astype(F32)
            return carry

        lax.fori_loop(0, depth, row_step, 0)


def face_terms(face_inverse, at, near, far, count):
    from_near = lookup(face_inverse[0, at, :], FACE_ROWS, lambda d, row: near[pl.ds(d * 16 + row, 1), :], count)
    from_far = lookup(face_inverse[1, at, :], FACE_ROWS, lambda d, row: far[pl.ds(d * 16 + row, 1), :], count)
    keep = has_far_face()
    return [from_near[d] + from_far[d] * keep for d in range(count)]


def gather_corners(scaled, corners):
    for d in range(3):
        for plane in range(4):
            shifted = corner_planes(scaled[d, pl.ds(plane * 8, 8), :], scaled[d, pl.ds(MAIN_ROWS + plane, 1), :])
            for up in range(2):
                layer = plane - up
                if 0 <= layer < 3:
                    for c in range(4):
                        corners[d, pl.ds(layer * 64 + up * 4 + c, 8, stride=8), :] = shifted[c]


def assemble(spread, misfit_grid, section, partial):
    for d in range(3):
        edges = []
        for plane in range(4):
            terms = []
            for c in range(4):
                total = None
                for up in range(2):
                    layer = plane - up
                    if 0 <= layer < 3:
                        term = spread[d, pl.ds(layer * 64 + up * 4 + c, 8, stride=8), :]
                        total = term if total is None else total + term
                terms.append(total)
            main, edge = assemble_plane(*terms)
            at = pl.ds(plane * 8, 8)
            partial[d, at, :] = main + misfit_grid[section, d, at, :]
            edges.append(edge)
        at = pl.ds(MAIN_ROWS, 8)
        edges = jnp.concatenate(edges + [jnp.zeros((4, LANES), F32)], axis=0)
        partial[d, at, :] = edges + misfit_grid[section, d, at, :]


PITCH = 9
TOGETHER = 2


def element_sweep(section, load, weigh, wide_map, softness, stiffness, decay, stored, internal, corners,
                  keep, internal_out, spread, weight, sums, rows, forcing_out=None):
    def tile_step(tile, slot):
        lanes = pl.ds(pl.multiple_of(tile * LANES, LANES), LANES)
        here = pl.ds(pl.multiple_of(tile * 8, 8), 8)
        scaled = [corners[d, here, :] for d in range(3)]
        total = [jnp.zeros((8, LANES), F32) for _ in range(3)]
        heavy = jnp.zeros((8, LANES), F32)
        for block in range(6):
            for i in range(8):
                lines = wide_map[tile, pl.ds((block * 8 + i) * 24, 24), :]
                sums[slot * 6 + block][pl.ds(i * PITCH, 8), :] = (
                    lines[0:8] * scaled[0] + lines[8:16] * scaled[1] + lines[16:24] * scaled[2]
                )
            product = sums[slot * 6 + block][pl.ds(0, 8, stride=PITCH), :]
            for i in range(1, 8):
                product = product + sums[slot * 6 + block][pl.ds(i, 8, stride=PITCH), :]
            rows_here = pl.ds(block * 8, 8)
            held = internal[rows_here, lanes]
            if keep is not None:
                held = held * keep
            forcing = decay[section, rows_here, lanes] * held - stiffness[rows_here, lanes] * product
            if weigh:
                heavy = heavy + forcing * stored[rows_here, lanes].astype(F32)
            if forcing_out is not None:
                internal_out[rows_here, lanes] = held - forcing
                forcing_out[rows_here, lanes] = forcing
            if load:
                internal_out[rows_here, lanes] = held - forcing
                rows[slot * 6 + block][...] = forcing
                for i in range(8):
                    lines = wide_map[tile, pl.ds((block * 8 + i) * 24, 24), :]
                    row = spread_row(rows[slot * 6 + block][pl.ds(i, 1), :])
                    for d in range(3):
                        total[d] = total[d] + lines[d * 8 : d * 8 + 8] * row
        if load:
            for d in range(3):
                spread[d, here, :] = total[d]
        if weigh:
            weight[pl.ds(tile, 1), :] = jnp.sum(heavy, axis=0, keepdims=True)

    def tiles_step(step, carry):
        for slot in range(TOGETHER):
            tile_step(step * TOGETHER + slot, slot)
        return carry

    lax.fori_loop(0, TILES // TOGETHER, tiles_step, 0)
    if weigh:
        weight[...] = weight[...] * softness[...]


def spread_sweep(wide_map, forcing, spread):
    def tiles_step(step, carry):
        for slot in range(TOGETHER):
            tile = step * TOGETHER + slot
            lanes = pl.ds(pl.multiple_of(tile * LANES, LANES), LANES)
            total = [jnp.zeros((8, LANES), F32) for _ in range(3)]
            for r in range(STRAIN):
                row = spread_row(forcing[pl.ds(r, 1), lanes])
                for d in range(3):
                    total[d] = total[d] + wide_map[tile, pl.ds(r * 24 + d * 8, 8), :] * row
            for d in range(3):
                spread[d, pl.ds(pl.multiple_of(tile * 8, 8), 8), :] = total[d]
        return carry

    lax.fori_loop(0, TILES // TOGETHER, tiles_step, 0)


def send_faces(face_position, partial, near, far):
    found = [
        lookup(face_position[pl.ds(block * 8, 8), :], GRID_ROWS, lambda d, row: partial[d, pl.ds(row, 1), :], 3)
        for block in range(3)
    ]
    put_faces(found, near, far, 3)


def sum_faces(own, face_inverse, near, far, put):
    for block in range(5):
        at = pl.ds(block * 8, 8)
        extra = face_terms(face_inverse, at, near, far, 3)
        for d in range(3):
            put(d, at, own[d, at, :] + extra[d])


def send_step(nodal, spread, misfit_grid, section, face_position, partial, own, near, far):
    assemble(spread, misfit_grid, section, partial)
    for d in range(3):
        own[d] = nodal[d] + partial[d]
    send_faces(face_position, partial, near, far)


def first_kernel(mass_grid, near, far, face_inverse, face_position, table, nodal, internal, wide_map,
                 stiffness, decay, misfit_grid,
                 inverse_mass, own, near_out, far_out, internal_out,
                 partial, scaled, corners, spread, sums, rows):
    for block in range(5):
        at = pl.ds(block * 8, 8)
        mass = mass_grid[at, :] + face_terms(face_inverse, at, near, far, 1)[0]
        inverse = 1.0 / jnp.where(table[at, :] < 0, 1.0, mass)
        inverse_mass[at, :] = inverse
        for d in range(3):
            scaled[d, at, :] = nodal[d, at, :] * inverse
    gather_corners(scaled, corners)
    element_sweep(1, True, False, wide_map, None, stiffness, decay, None, internal, corners, has_earlier_state(),
                  internal_out, spread, None, sums, rows)
    send_step(nodal, spread, misfit_grid, 1, face_position, partial, own, near_out, far_out)


def second_kernel(own_in, near, far, face_inverse, inverse_mass, internal,
                  wide_map, stiffness, decay, stored_in,
                  nodal, forcing, internal_out, stored, scaled, corners, sums, arrived):
    copies = fetch((stored_in,), (stored,), arrived)

    def put(d, at, value):
        nodal[d, at, :] = value
        scaled[d, at, :] = value * inverse_mass[at, :]

    sum_faces(own_in, face_inverse, near, far, put)
    gather_corners(scaled, corners)
    element_sweep(0, False, False, wide_map, None, stiffness, decay, None, internal, corners, None,
                  internal_out, None, None, sums, None, forcing)
    copies[0].wait()


def second_load_kernel(nodal, forcing, wide_map, misfit_grid, face_position, own, near_out, far_out, partial, spread):
    spread_sweep(wide_map, forcing, spread)
    send_step(nodal, spread, misfit_grid, 0, face_position, partial, own, near_out, far_out)


def third_kernel(own_in, near, far, face_inverse, face_position, inverse_mass, internal, wide_map, softness, stiffness,
                 decay, stored, misfit_grid, coarse_internal,
                 coarse, own, near_out, far_out, internal_out, weight, coarse_internal_out,
                 partial, scaled, corners, spread, sums, rows, nodal, arrived):
    copies = fetch((coarse_internal,), (coarse_internal_out,), arrived)
    keep = has_earlier_state()

    def put(d, at, value):
        coarse[d, at, :] = value
        nodal[d, at, :] = value * keep
        scaled[d, at, :] = value * (inverse_mass[at, :] * keep)

    sum_faces(own_in, face_inverse, near, far, put)
    gather_corners(scaled, corners)
    element_sweep(1, True, True, wide_map, softness, stiffness, decay, stored.at[1], internal, corners, keep,
                  internal_out, spread, weight, sums, rows)
    send_step(nodal, spread, misfit_grid, 1, face_position, partial, own, near_out, far_out)
    copies[0].wait()


def last_kernel(own, near, far, face_inverse, inverse_mass, internal, wide_map, softness,
                stiffness, decay, stored, weight_in, coarse, fine, weight, fine_internal, scaled, corners, sums, arrived):
    copies = fetch((internal,), (fine_internal,), arrived)

    def put(d, at, value):
        fine[d, at, :] = value
        scaled[d, at, :] = value * inverse_mass[at, :]

    sum_faces(own, face_inverse, near, far, put)
    gather_corners(scaled, corners)
    element_sweep(0, False, True, wide_map, softness, stiffness, decay, stored.at[0], internal, corners, None,
                  None, None, weight, sums, None)
    weight[...] = weight[...] + weight_in[...]
    copies[0].wait()


def local_kernel(inverse, coarse, fine, coarse_nodal, fine_nodal, found_rows):
    for grid, nodal in ((coarse, coarse_nodal), (fine, fine_nodal)):
        for block in range(5):
            at = pl.ds(block * 8, 8)
            found = lookup(inverse[at, :], GRID_ROWS, lambda d, row: grid[d, pl.ds(row, 1), :], 3)
            for d in range(3):
                found_rows[d, at, :] = found[d]
        for d in range(3):
            for row in range(NODE_ROWS):
                width = min(LANES, NODES - row * LANES)
                nodal[d, :, row * LANES : row * LANES + width] = found_rows[d, pl.ds(row, 1), :width]


def shape(*dims, dtype=F32):
    return jax.ShapeDtypeStruct(dims, dtype)


def call(kernel, outs, scratch, *operands, name=None, specs=None, limit=VMEM_LIMIT, to_hbm=()):
    if specs:
        operands = [
            pltpu.with_memory_space_constraint(operand, pltpu.HBM) if spec is HBM else operand
            for operand, spec in zip(operands, specs)
        ]
    return pl.pallas_call(
        kernel,
        in_specs=specs or [VMEM] * len(operands),
        out_specs=[HBM if i in to_hbm else VMEM for i in range(len(outs))] if isinstance(outs, tuple) else VMEM,
        out_shape=outs,
        scratch_shapes=scratch,
        compiler_params=pltpu.CompilerParams(vmem_limit_bytes=limit),
        name=name,
    )(*operands)


NODAL = (3, ROWS, LANES)
FACES = (48, LANES)


def vm(*dims, dtype=F32):
    return pltpu.VMEM(dims, dtype)


def exchange(near, far, back=0):
    windows, count = lax.axis_size("tm"), lax.axis_size("space")
    near_pairs, far_pairs = [], []
    for window in range(windows):
        for place in range(count):
            source, target = window * count + place, (window - back) % windows * count
            near_pairs.append((source, target + (place ^ 1)))
            other = place + 1 if place % 2 else place - 1
            if not 0 <= other < count:
                other, target = place, target if back else (window ^ 1) * count
            far_pairs.append((source, target + other))
    axes = ("tm", "space")
    far = lax.ppermute(far, axes, far_pairs)
    return lax.ppermute(near, axes, near_pairs), far


def to_earlier(block):
    count = lax.axis_size("tm")
    return lax.ppermute(block, "tm", [((i + 1) % count, i) for i in range(count)])


def to_later(block):
    count = lax.axis_size("tm")
    return lax.ppermute(block, "tm", [(i, (i + 1) % count) for i in range(count)])


def sum_windows(value):
    count = lax.axis_size("tm")
    value = value + lax.ppermute(value, "tm", [(i, i ^ 1) for i in range(count)])
    return value + lax.ppermute(value, "tm", [(i, i ^ 2) for i in range(count)])


def per_device(connect, low_face, up_face, strain_map, modulus, fluidity, element_mass, forward_strain, active, misfit,
               point_nodal, point_internal):
    modulus = modulus.reshape(TILES, LANES)
    fluidity = fluidity.reshape(TILES, LANES)
    mass = element_mass.reshape(TILES, LANES)
    nodal = to_earlier(jnp.transpose(point_nodal, (1, 0, 2)))
    internal = to_earlier(point_internal[0])
    elements = TILES * LANES
    table, inverse, face_position, mass_grid, near, far = call(
        tables_kernel,
        (shape(ROWS, LANES, dtype=I32), shape(ROWS, LANES, dtype=I32), shape(24, LANES, dtype=I32),
         shape(ROWS, LANES), shape(16, LANES), shape(16, LANES)),
        [vm(TILES * 8, LANES), vm(ROWS, LANES), vm(24, LANES, dtype=I32), vm(*connect.shape, dtype=I32),
         vm(*low_face.shape, dtype=I32), vm(*up_face.shape, dtype=I32), vm(TILES, LANES), pltpu.SemaphoreType.DMA((4,))],
        connect, low_face, up_face, mass, name="tables", specs=[HBM] * 4,
    )
    near, far = exchange(near, far)
    wide_map, stiffness, decay, softness = call(
        widen_kernel,
        (shape(TILES, STRAIN * 24, LANES), shape(STRAIN, elements), shape(2, STRAIN, elements), shape(TILES, LANES)),
        [vm(CHUNKS, STRAIN // CHUNKS, 24, elements, dtype=jnp.bfloat16), vm(TILES, LANES), vm(TILES, LANES),
         vm(*active.shape, dtype=I32), pltpu.SemaphoreType.DMA((CHUNKS,)), pltpu.SemaphoreType.DMA((3,))],
        strain_map, modulus, fluidity, active, name="widen", specs=[HBM] * 4, limit=20 * 1024 * 1024,
    )
    misfit_grid, face_inverse, nodal = call(
        loads_kernel, (shape(2, *NODAL), shape(2, ROWS, LANES, dtype=I32), shape(*NODAL)), [vm(*NODAL), vm(3, 2, NODES), pltpu.SemaphoreType.DMA((1,))],
        table, face_position, jnp.transpose(misfit, (1, 0, 2)), nodal, name="loads", specs=[VMEM, VMEM, HBM, VMEM],
    )
    sums = [vm(72, LANES) for _ in range(6 * TOGETHER)]
    work = [vm(*NODAL), vm(*NODAL), vm(3, TILES * 8, LANES), vm(3, TILES * 8, LANES), sums,
            [vm(8, LANES) for _ in range(6 * TOGETHER)]]
    more = [vm(*NODAL), pltpu.SemaphoreType.DMA((1,))]
    sent = (shape(*NODAL), shape(*FACES), shape(*FACES), shape(STRAIN, elements))
    inverse_mass, own, near, far, internal = call(
        first_kernel, (shape(ROWS, LANES),) + sent, work,
        mass_grid, near, far, face_inverse, face_position, table, nodal, internal, wide_map,
        stiffness, decay, misfit_grid, name="first",
    )
    near, far = exchange(near, far)
    nodal, forcing, internal, stored = call(
        second_kernel,
        (shape(*NODAL), shape(STRAIN, elements), shape(STRAIN, elements), shape(*forward_strain.shape, dtype=jnp.bfloat16)),
        [vm(*NODAL), vm(3, TILES * 8, LANES), sums, pltpu.SemaphoreType.DMA((1,))],
        own, near, far, face_inverse, inverse_mass, internal, wide_map, stiffness, decay, forward_strain,
        name="second", specs=[VMEM] * 9 + [HBM],
    )
    earlier = to_earlier(internal)
    own, near, far = call(
        second_load_kernel, (shape(*NODAL), shape(*FACES), shape(*FACES)), [vm(*NODAL), vm(3, TILES * 8, LANES)],
        nodal, forcing, wide_map, misfit_grid, face_position, name="second_load",
    )
    near, far = exchange(near, far, 1)
    own = to_earlier(own)

    coarse, own, near, far, held, weight, coarse_internal = call(
        third_kernel, (shape(*NODAL),) + sent + (shape(TILES, LANES), shape(STRAIN, elements)), work + more,
        own, near, far, face_inverse, face_position, inverse_mass, earlier, wide_map, softness, stiffness, decay, stored,
        misfit_grid, internal, name="third", to_hbm=(6,),
    )
    near, far = exchange(near, far)
    coarse = to_later(coarse)
    fine, weight, fine_internal = call(
        last_kernel, (shape(*NODAL), shape(TILES, LANES), shape(STRAIN, elements)),
        [vm(*NODAL), vm(3, TILES * 8, LANES), sums, pltpu.SemaphoreType.DMA((1,))],
        own, near, far, face_inverse, inverse_mass, held, wide_map, softness,
        stiffness, decay, stored, weight, coarse, name="last", to_hbm=(2,),
    )
    sensitivity = sum_windows(weight)
    coarse_nodal, fine_nodal = call(
        local_kernel, (shape(3, 1, NODES), shape(3, 1, NODES)), [vm(*NODAL)], inverse, coarse, fine, name="local"
    )
    coarse_nodal, fine_nodal = jnp.transpose(coarse_nodal, (1, 0, 2)), jnp.transpose(fine_nodal, (1, 0, 2))
    return coarse_nodal, coarse_internal[None], fine_nodal, fine_internal[None], sensitivity.reshape(-1)


def solution(mesh):
    in_specs = (
        P(None, "space"), P("space"), P("space"), P(None, None, "space"), P("space"), P("space"), P("space"),
        P("tm", None, "space"), P("tm", None, "space"), P("tm", None, "space"), P("tm", None, "space"),
        P("tm", None, "space"),
    )
    out_specs = (
        P("tm", None, "space"), P("tm", None, "space"), P("tm", None, "space"), P("tm", None, "space"), P("space"),
    )
    return jax.shard_map(per_device, mesh=mesh, in_specs=in_specs, out_specs=out_specs, check_vma=False)
```

```python
import jax
import jax.numpy as jnp
from jax import lax
from jax.experimental import pallas as pl
from jax.experimental.pallas import tpu as pltpu
from jax.sharding import PartitionSpec as P

LANES = 128
TILES = 24
STRAIN = 48
MAIN_ROWS = 32
GRID_ROWS = 36
ROWS = 40
NODES = 4356
NODE_ROWS = 35
FACE_ROWS = 9
VMEM_LIMIT = 12 * 1024 * 1024

VMEM = pl.BlockSpec(memory_space=pltpu.VMEM)
HBM = pl.BlockSpec(memory_space=pltpu.HBM)
F32 = jnp.float32
I32 = jnp.int32


def fetch(sources, targets, arrived):
    copies = [pltpu.make_async_copy(source, target, arrived.at[i]) for i, (source, target) in enumerate(zip(sources, targets))]
    for copy in copies:
        copy.start()
    return copies


def lane_ids():
    return lax.broadcasted_iota(I32, (8, LANES), 1)


def row_ids():
    return lax.broadcasted_iota(I32, (8, LANES), 0)


def roll(value, shift, axis):
    return pltpu.roll(value, shift % value.shape[axis], axis)


def spread_row(row):
    return jnp.broadcast_to(row, (8, LANES))


def pick(row, lanes):
    return jnp.take_along_axis(spread_row(row), lanes, axis=1)


def lookup(index, rows, row_of, count):
    high, low = index >> 7, index & 127
    found = [jnp.zeros((8, LANES), F32) for _ in range(count)]
    for row in range(rows):
        hit = high == row
        for d in range(count):
            found[d] = jnp.where(hit, pick(row_of(d, row), low), found[d])
    return found


def edge_row(at_x, at_y, at_xy):
    lane, row = lane_ids(), row_ids()
    along_x = jnp.take_along_axis(at_x, (lane & 3) * 32 + 31, axis=1)
    picked = jnp.where((row == (lane >> 2)) & (lane < 32), along_x, 0.0)
    picked = jnp.where((row == 7) & (lane >= 32) & (lane < 64), roll(at_y, -64, 1), picked)
    picked = jnp.where((row == 7) & (lane == 64), roll(at_xy, -63, 1), picked)
    return jnp.sum(picked, axis=0, keepdims=True)


def step_up_x(value):
    return jnp.where((lane_ids() & 31) == 0, 0.0, roll(value, 1, 1))


def step_up_y(value):
    turned = roll(value, 32, 1)
    below = jnp.where(row_ids() == 0, 0.0, roll(turned, 1, 0))
    return jnp.where(lane_ids() < 32, below, turned)


def assemble_plane(t00, t01, t10, t11):
    first = t00 + step_up_x(t01)
    second = t10 + step_up_x(t11)
    main = first + step_up_y(second)
    return main, edge_row(t01 + step_up_y(t11), second, t11)


def corner_planes(main, edge):
    lane, row = lane_ids(), row_ids()
    edge = spread_row(edge)
    along_x = jnp.take_along_axis(edge, row * 4 + (lane >> 5), axis=1)
    moved_x = jnp.where((lane & 31) == 31, along_x, roll(main, -1, 1))

    def move_y(value, last):
        turned = roll(value, -32, 1)
        above = jnp.where(row == 7, last, roll(turned, -1, 0))
        return jnp.where(lane < 96, turned, above)

    return main, moved_x, move_y(main, roll(edge, 64, 1)), move_y(moved_x, roll(edge, 63, 1))


def even_place():
    return lax.axis_index("space") % 2 == 0


def has_earlier_state():
    return jnp.where(lax.axis_index("tm") < lax.axis_size("tm") - 1, 1.0, 0.0)


def has_far_face():
    place = lax.axis_index("space")
    return jnp.where((place > 0) & (place < lax.axis_size("space") - 1), 1.0, 0.0)


def tables_kernel(connect_in, low_in, up_in, mass_in, table, inverse, face_position, mass_grid, mass_near, mass_far,
                  flat, numbers, faces, connect, low_face, up_face, mass, arrived):
    copies = fetch((connect_in, low_in, up_in, mass_in), (connect, low_face, up_face, mass), arrived)
    even = even_place()
    faces[...] = jnp.full((24, LANES), -1, I32)
    for copy in copies:
        copy.wait()
    for row in range(FACE_ROWS):
        width = min(LANES, low_face.shape[0] - row * LANES)
        at = slice(row * LANES, row * LANES + width)
        low, up = low_face[at], up_face[at]
        near, far = jnp.where(even, up, low), jnp.where(even, low, up)
        to = (row, row + 8) if row < 8 else (16, 17)
        faces[to[0], :width] = near
        faces[to[1], :width] = far
    for tile in range(TILES):
        flat[pl.ds(tile * 8, 8), :] = connect[:, tile * LANES : (tile + 1) * LANES].astype(F32)
    for plane in range(4):
        base, shift = (plane, 0) if plane < 3 else (2, 4)

        def corner(c):
            return flat[pl.ds(base * 64 + shift + c, 8, stride=8), :]

        numbers[pl.ds(plane * 8, 8), :] = corner(0)
        numbers[pl.ds(MAIN_ROWS + plane, 1), :] = edge_row(corner(1), corner(2), corner(3))
        below = mass[pl.ds((plane - 1) * 8, 8), :] if plane > 0 else 0.0
        above = mass[pl.ds(plane * 8, 8), :] if plane < 3 else 0.0
        both = (below + above) / 8.0
        main, edge = assemble_plane(both, both, both, both)
        mass_grid[pl.ds(plane * 8, 8), :] = main
        mass_grid[pl.ds(MAIN_ROWS + plane, 1), :] = edge
    numbers[pl.ds(GRID_ROWS, 4), :] = jnp.full((4, LANES), -1.0, F32)
    mass_grid[pl.ds(GRID_ROWS, 4), :] = jnp.zeros((4, LANES), F32)
    edges = numbers[pl.ds(MAIN_ROWS, 8), :]
    numbers[pl.ds(MAIN_ROWS, 8), :] = jnp.where((lane_ids() > 64) | (row_ids() > 3), -1.0, edges)
    table[...] = numbers[...].astype(I32)

    rows_at = lax.broadcasted_iota(I32, (ROWS, LANES), 0)
    lanes_at = lax.broadcasted_iota(I32, (LANES, LANES), 0)
    own_lane = lax.broadcasted_iota(I32, (ROWS, LANES), 1).astype(F32)
    found = jnp.zeros((2 * ROWS, LANES), F32)
    for row in range(GRID_ROWS):
        index = table[pl.ds(row, 1), :]
        hit = jnp.broadcast_to(index >> 7, (ROWS, LANES)) == rows_at
        left = jnp.concatenate([jnp.where(hit, float(row), 0.0), jnp.where(hit, own_lane, 0.0)], axis=0)
        right = jnp.where(jnp.broadcast_to(index & 127, (LANES, LANES)) == lanes_at, 1.0, 0.0)
        found = found + lax.dot_general(
            left.astype(jnp.bfloat16), right.astype(jnp.bfloat16), (((1,), (1,)), ((), ())), preferred_element_type=F32
        )
    numbers[...] = found[:ROWS] * 128.0 + found[ROWS:]
    inverse[...] = numbers[...].astype(I32)

    found = []
    for block in range(3):
        at = pl.ds(block * 8, 8)
        local = faces[at, :]
        position = lookup(local, NODE_ROWS, lambda d, row: numbers[pl.ds(row, 1), :], 1)[0]
        position = jnp.where(local < 0, -1, position.astype(I32))
        face_position[at, :] = position
        found.append(lookup(position, GRID_ROWS, lambda d, row: mass_grid[pl.ds(row, 1), :], 1))
    put_faces(found, mass_near, mass_far, 1)


def put_faces(found, near, far, count):
    for d in range(count):
        near[pl.ds(d * 16, 8), :] = found[0][d]
        near[pl.ds(d * 16 + 8, 8), :] = found[2][d]
        far[pl.ds(d * 16, 8), :] = found[1][d]
        far[pl.ds(d * 16 + 8, 8), :] = roll(found[2][d], -1, 0)


def local_to_grid(source, local, rows, table, put):
    for d in range(3):
        source[d, pl.ds(32, 8), :] = jnp.zeros((8, LANES), F32)
        for row in range(NODE_ROWS):
            width = min(LANES, NODES - row * LANES)
            source[d, pl.ds(row, 1), :width] = local[d, rows, row * LANES : row * LANES + width]
    for block in range(5):
        at = pl.ds(block * 8, 8)
        put(at, lookup(table[at, :], NODE_ROWS, lambda d, row: source[d, pl.ds(row, 1), :], 3))


def loads_kernel(table, face_position, misfit_in, nodal, misfit_grid, face_inverse, nodal_grid, source, misfit, arrived):
    copies = fetch((misfit_in,), (misfit,), arrived)
    keep = has_earlier_state()

    def put_nodal(at, found):
        for d in range(3):
            nodal_grid[d, at, :] = found[d] * keep

    local_to_grid(source, nodal, pl.ds(0, 1), table, put_nodal)
    copies[0].wait()
    for section in range(2):

        def put(at, found):
            for d in range(3):
                misfit_grid[section, d, at, :] = found[d]

        local_to_grid(source, misfit, pl.ds(section, 1), table, put)
    rows_at = lax.broadcasted_iota(I32, (ROWS, LANES), 0)
    lanes_at = lax.broadcasted_iota(I32, (LANES, LANES), 0)
    own_lane = lax.broadcasted_iota(I32, (ROWS, LANES), 1).astype(F32)
    for side in range(2):
        found = jnp.zeros((2 * ROWS, LANES), F32)
        for row in range(FACE_ROWS):
            index = face_position[pl.ds(row + side * 8 if row < 8 else 16 + side, 1), :]
            hit = jnp.broadcast_to(index >> 7, (ROWS, LANES)) == rows_at
            left = jnp.concatenate([jnp.where(hit, float(row + 1), 0.0), jnp.where(hit, own_lane, 0.0)], axis=0)
            right = jnp.where(jnp.broadcast_to(index & 127, (LANES, LANES)) == lanes_at, 1.0, 0.0)
            found = found + lax.dot_general(
                left.astype(jnp.bfloat16), right.astype(jnp.bfloat16), (((1,), (1,)), ((), ())), preferred_element_type=F32
            )
        face_inverse[side] = ((found[:ROWS] - 1.0) * 128.0 + found[ROWS:]).astype(I32)


CHUNKS = 3


def widen_kernel(strain_map, modulus_in, fluidity_in, active_in, wide_map, stiffness, decay, softness,
                 narrow, modulus, fluidity, active, arrived, small_arrived):
    depth = STRAIN // CHUNKS
    small = fetch((modulus_in, fluidity_in, active_in), (modulus, fluidity, active), small_arrived)
    copies = fetch(
        [strain_map.at[pl.ds(part * depth, depth)] for part in range(CHUNKS)], [narrow.at[part] for part in range(CHUNKS)], arrived
    )
    for copy in small:
        copy.wait()
    softness[...] = 1.0 / modulus[...]

    def tile_step(tile, carry):
        lanes = pl.ds(pl.multiple_of(tile * LANES, LANES), LANES)
        own = spread_row(modulus[pl.ds(tile, 1), :])
        rates = [active[n, :, lanes].astype(F32) * fluidity[pl.ds(tile, 1), :] for n in range(2)]
        for block in range(6):
            row = row_ids() + block * 8
            here = jnp.where(row % 6 < 3, 2.0, 1.0) * own
            stiffness[pl.ds(block * 8, 8), lanes] = here
            point = block * 8 // 6
            for n in range(2):
                rate = jnp.where(row < (point + 1) * 6, rates[n][point : point + 1], rates[n][point + 1 : point + 2])
                decay[n, pl.ds(block * 8, 8), lanes] = here * rate
        return carry

    lax.fori_loop(0, TILES, tile_step, 0)
    for part in range(CHUNKS):
        copies[part].wait()

        def row_step(row, carry):
            to = pl.ds(pl.multiple_of((part * depth + row) * 24, 8), 24)
            for tile in range(TILES):
                wide_map[tile, to, :] = narrow[part, row, :, tile * LANES : (tile + 1) * LANES].astype(F32)
            return carry

        lax.fori_loop(0, depth, row_step, 0)


def face_terms(face_inverse, at, near, far, count):
    from_near = lookup(face_inverse[0, at, :], FACE_ROWS, lambda d, row: near[pl.ds(d * 16 + row, 1), :], count)
    from_far = lookup(face_inverse[1, at, :], FACE_ROWS, lambda d, row: far[pl.ds(d * 16 + row, 1), :], count)
    keep = has_far_face()
    return [from_near[d] + from_far[d] * keep for d in range(count)]


def gather_corners(scaled, corners):
    for d in range(3):
        for plane in range(4):
            shifted = corner_planes(scaled[d, pl.ds(plane * 8, 8), :], scaled[d, pl.ds(MAIN_ROWS + plane, 1), :])
            for up in range(2):
                layer = plane - up
                if 0 <= layer < 3:
                    for c in range(4):
                        corners[d, pl.ds(layer * 64 + up * 4 + c, 8, stride=8), :] = shifted[c]


def assemble(spread, misfit_grid, section, partial):
    for d in range(3):
        edges = []
        for plane in range(4):
            terms = []
            for c in range(4):
                total = None
                for up in range(2):
                    layer = plane - up
                    if 0 <= layer < 3:
                        term = spread[d, pl.ds(layer * 64 + up * 4 + c, 8, stride=8), :]
                        total = term if total is None else total + term
                terms.append(total)
            main, edge = assemble_plane(*terms)
            at = pl.ds(plane * 8, 8)
            partial[d, at, :] = main + misfit_grid[section, d, at, :]
            edges.append(edge)
        at = pl.ds(MAIN_ROWS, 8)
        edges = jnp.concatenate(edges + [jnp.zeros((4, LANES), F32)], axis=0)
        partial[d, at, :] = edges + misfit_grid[section, d, at, :]


PITCH = 9
TOGETHER = 4


def element_sweep(section, load, weigh, wide_map, softness, stiffness, decay, stored, internal, corners,
                  keep, internal_out, spread, weight, sums, rows, forcing_out=None):
    def tile_step(tile, slot):
        lanes = pl.ds(pl.multiple_of(tile * LANES, LANES), LANES)
        here = pl.ds(pl.multiple_of(tile * 8, 8), 8)
        scaled = [corners[d, here, :] for d in range(3)]
        total = [jnp.zeros((8, LANES), F32) for _ in range(3)]
        heavy = jnp.zeros((8, LANES), F32)
        for block in range(6):
            for i in range(8):
                lines = wide_map[tile, pl.ds((block * 8 + i) * 24, 24), :]
                sums[slot * 6 + block][pl.ds(i * PITCH, 8), :] = (
                    lines[0:8] * scaled[0] + lines[8:16] * scaled[1] + lines[16:24] * scaled[2]
                )
            product = sums[slot * 6 + block][pl.ds(0, 8, stride=PITCH), :]
            for i in range(1, 8):
                product = product + sums[slot * 6 + block][pl.ds(i, 8, stride=PITCH), :]
            rows_here = pl.ds(block * 8, 8)
            held = internal[rows_here, lanes]
            if keep is not None:
                held = held * keep
            forcing = decay[section, rows_here, lanes] * held - stiffness[rows_here, lanes] * product
            if weigh:
                heavy = heavy + forcing * stored[rows_here, lanes].astype(F32)
            if forcing_out is not None:
                internal_out[rows_here, lanes] = held - forcing
                forcing_out[rows_here, lanes] = forcing
            if load:
                internal_out[rows_here, lanes] = held - forcing
                rows[slot * 6 + block][...] = forcing
                for i in range(8):
                    lines = wide_map[tile, pl.ds((block * 8 + i) * 24, 24), :]
                    row = spread_row(rows[slot * 6 + block][pl.ds(i, 1), :])
                    for d in range(3):
                        total[d] = total[d] + lines[d * 8 : d * 8 + 8] * row
        if load:
            for d in range(3):
                spread[d, here, :] = total[d]
        if weigh:
            weight[pl.ds(tile, 1), :] = jnp.sum(heavy, axis=0, keepdims=True)

    def tiles_step(step, carry):
        for slot in range(TOGETHER):
            tile_step(step * TOGETHER + slot, slot)
        return carry

    lax.fori_loop(0, TILES // TOGETHER, tiles_step, 0)
    if weigh:
        weight[...] = weight[...] * softness[...]


def spread_sweep(wide_map, forcing, spread):
    def tiles_step(step, carry):
        for slot in range(TOGETHER):
            tile = step * TOGETHER + slot
            lanes = pl.ds(pl.multiple_of(tile * LANES, LANES), LANES)
            total = [jnp.zeros((8, LANES), F32) for _ in range(3)]
            for r in range(STRAIN):
                row = spread_row(forcing[pl.ds(r, 1), lanes])
                for d in range(3):
                    total[d] = total[d] + wide_map[tile, pl.ds(r * 24 + d * 8, 8), :] * row
            for d in range(3):
                spread[d, pl.ds(pl.multiple_of(tile * 8, 8), 8), :] = total[d]
        return carry

    lax.fori_loop(0, TILES // TOGETHER, tiles_step, 0)


def send_faces(face_position, partial, near, far):
    found = [
        lookup(face_position[pl.ds(block * 8, 8), :], GRID_ROWS, lambda d, row: partial[d, pl.ds(row, 1), :], 3)
        for block in range(3)
    ]
    put_faces(found, near, far, 3)


def sum_faces(own, face_inverse, near, far, put):
    for block in range(5):
        at = pl.ds(block * 8, 8)
        extra = face_terms(face_inverse, at, near, far, 3)
        for d in range(3):
            put(d, at, own[d, at, :] + extra[d])


def send_step(nodal, spread, misfit_grid, section, face_position, partial, own, near, far):
    assemble(spread, misfit_grid, section, partial)
    for d in range(3):
        own[d] = nodal[d] + partial[d]
    send_faces(face_position, partial, near, far)


def first_kernel(mass_grid, near, far, face_inverse, face_position, table, nodal, internal, wide_map,
                 stiffness, decay, misfit_grid,
                 inverse_mass, own, near_out, far_out, internal_out,
                 partial, scaled, corners, spread, sums, rows):
    for block in range(5):
        at = pl.ds(block * 8, 8)
        mass = mass_grid[at, :] + face_terms(face_inverse, at, near, far, 1)[0]
        inverse = 1.0 / jnp.where(table[at, :] < 0, 1.0, mass)
        inverse_mass[at, :] = inverse
        for d in range(3):
            scaled[d, at, :] = nodal[d, at, :] * inverse
    gather_corners(scaled, corners)
    element_sweep(1, True, False, wide_map, None, stiffness, decay, None, internal, corners, has_earlier_state(),
                  internal_out, spread, None, sums, rows)
    send_step(nodal, spread, misfit_grid, 1, face_position, partial, own, near_out, far_out)


def second_kernel(own_in, near, far, face_inverse, inverse_mass, internal,
                  wide_map, stiffness, decay, stored_in,
                  nodal, forcing, internal_out, stored, scaled, corners, sums, arrived):
    copies = fetch((stored_in,), (stored,), arrived)

    def put(d, at, value):
        nodal[d, at, :] = value
        scaled[d, at, :] = value * inverse_mass[at, :]

    sum_faces(own_in, face_inverse, near, far, put)
    gather_corners(scaled, corners)
    element_sweep(0, False, False, wide_map, None, stiffness, decay, None, internal, corners, None,
                  internal_out, None, None, sums, None, forcing)
    copies[0].wait()


def second_load_kernel(nodal, forcing, wide_map, misfit_grid, face_position, own, near_out, far_out, partial, spread):
    spread_sweep(wide_map, forcing, spread)
    send_step(nodal, spread, misfit_grid, 0, face_position, partial, own, near_out, far_out)


def third_kernel(own_in, near, far, face_inverse, face_position, inverse_mass, internal, wide_map, softness, stiffness,
                 decay, stored, misfit_grid, coarse_internal,
                 coarse, own, near_out, far_out, internal_out, weight, coarse_internal_out,
                 partial, scaled, corners, spread, sums, rows, nodal, arrived):
    copies = fetch((coarse_internal,), (coarse_internal_out,), arrived)
    keep = has_earlier_state()

    def put(d, at, value):
        coarse[d, at, :] = value
        nodal[d, at, :] = value * keep
        scaled[d, at, :] = value * (inverse_mass[at, :] * keep)

    sum_faces(own_in, face_inverse, near, far, put)
    gather_corners(scaled, corners)
    element_sweep(1, True, True, wide_map, softness, stiffness, decay, stored.at[1], internal, corners, keep,
                  internal_out, spread, weight, sums, rows)
    send_step(nodal, spread, misfit_grid, 1, face_position, partial, own, near_out, far_out)
    copies[0].wait()


def last_kernel(own, near, far, face_inverse, inverse_mass, internal, wide_map, softness,
                stiffness, decay, stored, weight_in, coarse, fine, weight, fine_internal, scaled, corners, sums, arrived):
    copies = fetch((internal,), (fine_internal,), arrived)

    def put(d, at, value):
        fine[d, at, :] = value
        scaled[d, at, :] = value * inverse_mass[at, :]

    sum_faces(own, face_inverse, near, far, put)
    gather_corners(scaled, corners)
    element_sweep(0, False, True, wide_map, softness, stiffness, decay, stored.at[0], internal, corners, None,
                  None, None, weight, sums, None)
    weight[...] = weight[...] + weight_in[...]
    copies[0].wait()


def local_kernel(inverse, coarse, fine, coarse_nodal, fine_nodal, found_rows):
    for grid, nodal in ((coarse, coarse_nodal), (fine, fine_nodal)):
        for block in range(5):
            at = pl.ds(block * 8, 8)
            found = lookup(inverse[at, :], GRID_ROWS, lambda d, row: grid[d, pl.ds(row, 1), :], 3)
            for d in range(3):
                found_rows[d, at, :] = found[d]
        for d in range(3):
            for row in range(NODE_ROWS):
                width = min(LANES, NODES - row * LANES)
                nodal[d, :, row * LANES : row * LANES + width] = found_rows[d, pl.ds(row, 1), :width]


def shape(*dims, dtype=F32):
    return jax.ShapeDtypeStruct(dims, dtype)


def call(kernel, outs, scratch, *operands, name=None, specs=None, limit=VMEM_LIMIT, to_hbm=()):
    if specs:
        operands = [
            pltpu.with_memory_space_constraint(operand, pltpu.HBM) if spec is HBM else operand
            for operand, spec in zip(operands, specs)
        ]
    return pl.pallas_call(
        kernel,
        in_specs=specs or [VMEM] * len(operands),
        out_specs=[HBM if i in to_hbm else VMEM for i in range(len(outs))] if isinstance(outs, tuple) else VMEM,
        out_shape=outs,
        scratch_shapes=scratch,
        compiler_params=pltpu.CompilerParams(vmem_limit_bytes=limit),
        name=name,
    )(*operands)


NODAL = (3, ROWS, LANES)
FACES = (48, LANES)


def vm(*dims, dtype=F32):
    return pltpu.VMEM(dims, dtype)


def exchange(near, far, back=0):
    windows, count = lax.axis_size("tm"), lax.axis_size("space")
    near_pairs, far_pairs = [], []
    for window in range(windows):
        for place in range(count):
            source, target = window * count + place, (window - back) % windows * count
            near_pairs.append((source, target + (place ^ 1)))
            other = place + 1 if place % 2 else place - 1
            if not 0 <= other < count:
                other, target = place, target if back else (window ^ 1) * count
            far_pairs.append((source, target + other))
    axes = ("tm", "space")
    far = lax.ppermute(far, axes, far_pairs)
    return lax.ppermute(near, axes, near_pairs), far


def to_earlier(block):
    count = lax.axis_size("tm")
    return lax.ppermute(block, "tm", [((i + 1) % count, i) for i in range(count)])


def to_later(block):
    count = lax.axis_size("tm")
    return lax.ppermute(block, "tm", [(i, (i + 1) % count) for i in range(count)])


def sum_windows(value):
    count = lax.axis_size("tm")
    value = value + lax.ppermute(value, "tm", [(i, i ^ 1) for i in range(count)])
    return value + lax.ppermute(value, "tm", [(i, i ^ 2) for i in range(count)])


def per_device(connect, low_face, up_face, strain_map, modulus, fluidity, element_mass, forward_strain, active, misfit,
               point_nodal, point_internal):
    modulus = modulus.reshape(TILES, LANES)
    fluidity = fluidity.reshape(TILES, LANES)
    mass = element_mass.reshape(TILES, LANES)
    nodal = to_earlier(jnp.transpose(point_nodal, (1, 0, 2)))
    internal = to_earlier(point_internal[0])
    elements = TILES * LANES
    table, inverse, face_position, mass_grid, near, far = call(
        tables_kernel,
        (shape(ROWS, LANES, dtype=I32), shape(ROWS, LANES, dtype=I32), shape(24, LANES, dtype=I32),
         shape(ROWS, LANES), shape(16, LANES), shape(16, LANES)),
        [vm(TILES * 8, LANES), vm(ROWS, LANES), vm(24, LANES, dtype=I32), vm(*connect.shape, dtype=I32),
         vm(*low_face.shape, dtype=I32), vm(*up_face.shape, dtype=I32), vm(TILES, LANES), pltpu.SemaphoreType.DMA((4,))],
        connect, low_face, up_face, mass, name="tables", specs=[HBM] * 4,
    )
    near, far = exchange(near, far)
    wide_map, stiffness, decay, softness = call(
        widen_kernel,
        (shape(TILES, STRAIN * 24, LANES), shape(STRAIN, elements), shape(2, STRAIN, elements), shape(TILES, LANES)),
        [vm(CHUNKS, STRAIN // CHUNKS, 24, elements, dtype=jnp.bfloat16), vm(TILES, LANES), vm(TILES, LANES),
         vm(*active.shape, dtype=I32), pltpu.SemaphoreType.DMA((CHUNKS,)), pltpu.SemaphoreType.DMA((3,))],
        strain_map, modulus, fluidity, active, name="widen", specs=[HBM] * 4, limit=20 * 1024 * 1024,
    )
    misfit_grid, face_inverse, nodal = call(
        loads_kernel, (shape(2, *NODAL), shape(2, ROWS, LANES, dtype=I32), shape(*NODAL)), [vm(*NODAL), vm(3, 2, NODES), pltpu.SemaphoreType.DMA((1,))],
        table, face_position, jnp.transpose(misfit, (1, 0, 2)), nodal, name="loads", specs=[VMEM, VMEM, HBM, VMEM],
    )
    sums = [vm(72, LANES) for _ in range(6 * TOGETHER)]
    work = [vm(*NODAL), vm(*NODAL), vm(3, TILES * 8, LANES), vm(3, TILES * 8, LANES), sums,
            [vm(8, LANES) for _ in range(6 * TOGETHER)]]
    more = [vm(*NODAL), pltpu.SemaphoreType.DMA((1,))]
    sent = (shape(*NODAL), shape(*FACES), shape(*FACES), shape(STRAIN, elements))
    inverse_mass, own, near, far, internal = call(
        first_kernel, (shape(ROWS, LANES),) + sent, work,
        mass_grid, near, far, face_inverse, face_position, table, nodal, internal, wide_map,
        stiffness, decay, misfit_grid, name="first",
    )
    near, far = exchange(near, far)
    nodal, forcing, internal, stored = call(
        second_kernel,
        (shape(*NODAL), shape(STRAIN, elements), shape(STRAIN, elements), shape(*forward_strain.shape, dtype=jnp.bfloat16)),
        [vm(*NODAL), vm(3, TILES * 8, LANES), sums, pltpu.SemaphoreType.DMA((1,))],
        own, near, far, face_inverse, inverse_mass, internal, wide_map, stiffness, decay, forward_strain,
        name="second", specs=[VMEM] * 9 + [HBM],
    )
    earlier = to_earlier(internal)
    own, near, far = call(
        second_load_kernel, (shape(*NODAL), shape(*FACES), shape(*FACES)), [vm(*NODAL), vm(3, TILES * 8, LANES)],
        nodal, forcing, wide_map, misfit_grid, face_position, name="second_load",
    )
    near, far = exchange(near, far, 1)
    own = to_earlier(own)

    coarse, own, near, far, held, weight, coarse_internal = call(
        third_kernel, (shape(*NODAL),) + sent + (shape(TILES, LANES), shape(STRAIN, elements)), work + more,
        own, near, far, face_inverse, face_position, inverse_mass, earlier, wide_map, softness, stiffness, decay, stored,
        misfit_grid, internal, name="third", to_hbm=(6,),
    )
    near, far = exchange(near, far)
    coarse = to_later(coarse)
    fine, weight, fine_internal = call(
        last_kernel, (shape(*NODAL), shape(TILES, LANES), shape(STRAIN, elements)),
        [vm(*NODAL), vm(3, TILES * 8, LANES), sums, pltpu.SemaphoreType.DMA((1,))],
        own, near, far, face_inverse, inverse_mass, held, wide_map, softness,
        stiffness, decay, stored, weight, coarse, name="last", to_hbm=(2,),
    )
    sensitivity = sum_windows(weight)
    coarse_nodal, fine_nodal = call(
        local_kernel, (shape(3, 1, NODES), shape(3, 1, NODES)), [vm(*NODAL)], inverse, coarse, fine, name="local"
    )
    coarse_nodal, fine_nodal = jnp.transpose(coarse_nodal, (1, 0, 2)), jnp.transpose(fine_nodal, (1, 0, 2))
    return coarse_nodal, coarse_internal[None], fine_nodal, fine_internal[None], sensitivity.reshape(-1)


def solution(mesh):
    in_specs = (
        P(None, "space"), P("space"), P("space"), P(None, None, "space"), P("space"), P("space"), P("space"),
        P("tm", None, "space"), P("tm", None, "space"), P("tm", None, "space"), P("tm", None, "space"),
        P("tm", None, "space"),
    )
    out_specs = (
        P("tm", None, "space"), P("tm", None, "space"), P("tm", None, "space"), P("tm", None, "space"), P("space"),
    )
    return jax.shard_map(per_device, mesh=mesh, in_specs=in_specs, out_specs=out_specs, check_vma=False)
```
